32 devices in a mesh: row: 4 (over x, core), col: 8 (over z, y).
Axes of the slice: x: 2, y: 2, z: 4, core: 2. Of those that a mesh axis runs over, the one named last changes fastest.
Arguments:
- amplitudes: bfloat16 [2048, 16384], P(('row', 'col')), may hold values from -6 to 6
- integrals: bfloat16 [8192, 16384], P('col', 'row'), may hold values from -0.21875 to 0.21875
- orbital_irrep: int32 [1024], replicated, may hold values from 0 to 7
- orbital_spin: int32 [1024], replicated, may hold values from 0 to 1
Outputs:
- residual_tiles: bfloat16 [2048, 8192], P('row', 'col')
The draws below stay inside these ranges and needn't reach their ends.
All inputs are finite; a program needn't handle non-finite values.
Results may differ from the reference program's by a relative error of at most 0.001.
Values may be sent and summed in bfloat16 or wider, within the bound.
No kernel may reach another device: no remote copies, remote signals or barrier semaphores. Data moves between devices by JAX's collectives and lax.ppermute only.
A program may use at most 128 MiB of HBM per device.

```python
import jax
import jax.numpy as jnp
from jax import lax

NVIR = 1024
PAIRS = 2048
A_TOT = 8
C_TOT = 16
AB = 8192
CD = 16384


def touch_ends(entries, rng, least, largest):
    longest = entries.shape.index(max(entries.shape))
    spots = []
    for shift in (0, 1):
        where = [jax.random.randint(jax.random.fold_in(rng, axis), (), 0, length) for axis, length in enumerate(entries.shape)]
        where[longest] = (where[longest] + shift) % entries.shape[longest]
        spots.append(tuple(where))
    return entries.at[spots[0]].set(least).at[spots[1]].set(largest)


def level_of(key, shape, pieces, smallest, high):
    loudness, own = 1.0, jax.random.fold_in(key, 6)
    for axis_at, blocks in pieces:
        heights = jnp.exp(jax.random.uniform(jax.random.fold_in(own, axis_at), (blocks,), jnp.float32, smallest / len(pieces), high / len(pieces)))
        loudness = loudness * jnp.repeat(heights, shape[axis_at] // blocks).reshape([-1 if axis == axis_at else 1 for axis in range(len(shape))])
    return loudness


def scatter_about(key, shape, scale, most, split=(), held_as=jnp.bfloat16):
    drawn = scale * jax.random.normal(key, shape, jnp.float32)
    if split:
        drawn = drawn * level_of(key, shape, split, -0.22, 0.18)
    return jnp.clip(drawn, -most, most).astype(held_as)


def setup_inputs(seed: int = 0) -> dict:
    key_list = jax.random.split(jax.random.key(seed), 5)
    return {
        "amplitudes": scatter_about(key_list[0], (PAIRS, CD), 1.0, 6.0, ((0, 32),)),
        "integrals": scatter_about(key_list[1], (AB, CD), (CD // 20) ** -0.5, 0.21875, ((0, 8), (1, 4))),
        "orbital_irrep": touch_ends(jax.random.randint(key_list[2], (NVIR,), 0, 8), jax.random.fold_in(key_list[2], 1), 0, 7).astype(jnp.int32),
        "orbital_spin": touch_ends(jax.random.randint(key_list[3], (NVIR,), 0, 2), jax.random.fold_in(key_list[3], 1), 0, 1).astype(jnp.int32),
    }


def reference(amplitudes, integrals, orbital_irrep, orbital_spin):
    c_index = jnp.arange(C_TOT, dtype=jnp.int32)
    cd_labels = (jnp.bitwise_xor(orbital_irrep[c_index][:, None], orbital_irrep[None, :])
                 + 8 * (orbital_spin[c_index][:, None] + orbital_spin[None, :])).reshape(-1)
    table = amplitudes.astype(jnp.float32)

    def one_block(index):
        rows = lax.dynamic_slice_in_dim(integrals, (index * NVIR).astype(jnp.int32), NVIR, 0)
        ab_labels = jnp.bitwise_xor(orbital_irrep[index], orbital_irrep) + 8 * (orbital_spin[index] + orbital_spin)
        masked = jnp.where(ab_labels[:, None] == cd_labels[None, :], rows, jnp.zeros((), rows.dtype))
        return jnp.dot(table, masked.astype(jnp.float32).T, precision=lax.Precision.HIGHEST)

    blocks = lax.map(one_block, jnp.arange(A_TOT, dtype=jnp.int32))
    return blocks.transpose(1, 0, 2).reshape(PAIRS, A_TOT * NVIR).astype(jnp.bfloat16)
```

```python
import functools

import jax
import jax.numpy as jnp
from jax import lax
from jax.experimental import pallas as pl
from jax.experimental.pallas import tpu as pltpu
from jax.sharding import Mesh, PartitionSpec as P

IRREPS = 8
LANES = 128
NT = (((1,), (1,)), ((), ()))


def pair_labels(lead_irrep, lead_spin, irrep, spin):
    return jnp.bitwise_xor(lead_irrep[:, None], irrep[None, :]) + 8 * (
        lead_spin[:, None] + spin[None, :]
    )


def dense(amplitudes, integrals, irrep, spin):
    virtuals = irrep.shape[0]
    a_count = integrals.shape[0] // virtuals
    c_count = integrals.shape[1] // virtuals
    col = ("plane", "sub")

    def labels(first, count):
        return pair_labels(
            lax.dynamic_slice_in_dim(irrep, first, count, 0),
            lax.dynamic_slice_in_dim(spin, first, count, 0),
            irrep,
            spin,
        ).reshape(-1)

    ab_labels = labels(lax.axis_index(col) * a_count, a_count)
    cd_labels = labels(lax.axis_index("row") * c_count, c_count)
    masked = jnp.where(
        ab_labels[:, None] == cd_labels[None, :], integrals, jnp.zeros((), integrals.dtype)
    )
    grid_rows = lax.all_gather(amplitudes, col, axis=0, tiled=True)
    regrouped = lax.all_to_all(grid_rows, "row", split_axis=1, concat_axis=0, tiled=True)
    partial_sums = lax.dot_general(regrouped, masked, NT, preferred_element_type=jnp.float32)
    return lax.psum_scatter(partial_sums, "row", scatter_dimension=0, tiled=True).astype(
        jnp.bfloat16
    )


def pack_integrals_kernel(c_count, cap, row_label, cd_label, column_slot, row_slot, v_ref, out_ref):
    virtuals = v_ref.shape[0]
    front = None
    for c in range(c_count):
        block = v_ref[:, c * virtuals : (c + 1) * virtuals]
        keep = row_label[...] == cd_label[c : c + 1, :]
        masked = jnp.where(keep, block, jnp.zeros((), block.dtype))
        lane = lax.broadcasted_iota(jnp.int32, (virtuals, 384), 1)
        lane = jnp.where(lane >= 320, lane - 64, lane)
        place = (column_slot[:, c : c + 1] == lane).astype(jnp.bfloat16)
        term = jnp.dot(masked, place, preferred_element_type=jnp.float32)
        front = term if front is None else front + term
    front = front.astype(jnp.bfloat16)
    half = cap // 2
    for g in range(IRREPS):
        spot = lax.broadcasted_iota(jnp.int32, (cap, virtuals), 0) + g * cap
        rows = (row_slot[...] == spot).astype(jnp.bfloat16)
        packed = jnp.dot(rows, front, preferred_element_type=jnp.float32)
        left = lax.broadcasted_iota(jnp.int32, (half, LANES), 1) < 64
        tail = jnp.where(left, packed[:half, 256:], packed[half:, 256:])
        out_ref[g, :cap, :] = packed[:, :128].astype(jnp.bfloat16)
        out_ref[g, cap : 2 * cap, :] = packed[:, 128:256].astype(jnp.bfloat16)
        out_ref[g, 2 * cap :, :] = tail.astype(jnp.bfloat16)


def pack_amplitudes_kernel(c_total, cap, lead_irrep, slot, t_ref, out_ref, stacked, moved):
    pairs = t_ref.shape[0]
    virtuals = slot.shape[1]
    fold = LANES // pairs
    tiles = c_total // fold
    for j in range(tiles):
        for h in range(fold):
            c = h * tiles + j
            at = (j * fold + h) * pairs
            stacked[at : at + pairs, :] = t_ref[:, c * virtuals : (c + 1) * virtuals]
    for g in range(IRREPS):
        spot = lax.broadcasted_iota(jnp.int32, (cap, virtuals), 0) + g * cap
        rows = (slot[...] == spot).astype(jnp.bfloat16)
        moved[g] = lax.dot_general(
            rows, stacked[...], NT, preferred_element_type=jnp.float32
        ).astype(jnp.bfloat16)
    share = lax.broadcasted_iota(jnp.int32, (cap, LANES), 1) // pairs
    for g in range(IRREPS):
        for j in range(tiles):
            tile = None
            for h in range(fold):
                source = jnp.bitwise_xor(lead_irrep[h * tiles + j], g)
                part = moved[source, :, j * LANES : (j + 1) * LANES]
                tile = part if tile is None else jnp.where(share == h, part, tile)
            out_ref[g, j * cap : (j + 1) * cap, :] = tile


def contract_kernel(rows, subs, cap, lead_spin, low, target, t_ref, v_ref, out_ref, t_label, v_rows):
    plane = pl.program_id(0)
    half = cap // 2
    main = rows * 256
    wide = t_ref.shape[0] // rows

    @pl.when(plane == 0)
    def _():
        for s in range(3):
            for r in range(rows):
                spot = lax.broadcasted_iota(jnp.int32, (384, wide), 0)
                spot = jnp.where(spot >= 320, spot - 64, spot)
                place = (target[s * rows + r : s * rows + r + 1, :] == spot).astype(jnp.bfloat16)
                part = jnp.dot(
                    place, t_ref[r * wide : (r + 1) * wide, :], preferred_element_type=jnp.float32
                ).astype(jnp.bfloat16)
                t_label[s, r * 256 : (r + 1) * 256, :] = part[:256]
                t_label[s, main + r * 128 : main + (r + 1) * 128, :] = part[256:]

    for y in range(subs):
        for r in range(rows):
            source = r * subs + y
            v_rows[:, r * 256 : r * 256 + 128] = v_ref[0, source, :cap, :]
            v_rows[:, r * 256 + 128 : (r + 1) * 256] = v_ref[0, source, cap : 2 * cap, :]
            tail = v_ref[0, source, 2 * cap :, :]
            left = lax.broadcasted_iota(jnp.int32, (half, LANES), 1) < 64
            none = jnp.zeros((), tail.dtype)
            at = main + r * 128
            v_rows[:half, at : at + 128] = jnp.where(left, tail, none)
            v_rows[half:, at : at + 128] = jnp.where(left, none, tail)
        a = plane * subs + y
        s = lead_spin[a]
        first = jnp.dot(v_rows[...], t_label[s], preferred_element_type=jnp.float32)
        second = jnp.dot(v_rows[...], t_label[s + 1], preferred_element_type=jnp.float32)
        upper = lax.broadcasted_iota(jnp.int32, first.shape, 0) < low[a]
        result = jnp.where(upper, first, second).astype(jnp.bfloat16)
        pairs = result.shape[1] // rows
        for r in range(rows):
            out_ref[r, 0, y] = result[:, r * pairs : (r + 1) * pairs]


def in_vmem(limit=48):
    return pltpu.CompilerParams(vmem_limit_bytes=limit * 2**20)


VMEM = pl.BlockSpec(memory_space=pltpu.VMEM)
SMEM = pl.BlockSpec(memory_space=pltpu.SMEM)


def packed(rows, planes, subs, amplitudes, integrals, irrep, spin, ranks, counts, offsets):
    virtuals = irrep.shape[0]
    c_count = integrals.shape[1] // virtuals
    c_total = amplitudes.shape[1] // virtuals
    a_total = planes * subs
    pairs = amplitudes.shape[0]
    cap = virtuals // IRREPS * 5 // 4
    row, plane, sub = (lax.axis_index(n) for n in ("row", "plane", "sub"))
    mine = row * subs + sub
    a = plane * subs + sub
    a_irrep = lax.dynamic_index_in_dim(irrep, a, keepdims=False)
    a_spin = lax.dynamic_index_in_dim(spin, a, keepdims=False)

    row_label = jnp.bitwise_xor(a_irrep, irrep) + 8 * (a_spin + spin)
    cd_label = pair_labels(
        lax.dynamic_slice_in_dim(irrep, row * c_count, c_count),
        lax.dynamic_slice_in_dim(spin, row * c_count, c_count),
        irrep,
        spin,
    )
    my_offsets = lax.dynamic_index_in_dim(offsets, row, keepdims=False)
    labels = jnp.arange(24, dtype=jnp.int32)
    rank16 = ranks[0]
    column_slot = rank16[None, :] + jnp.sum(
        jnp.where(cd_label[:, :, None] == labels, my_offsets[:, None, :], 0), axis=2
    )
    row_slot = jnp.bitwise_xor(irrep, a_irrep) * cap + ranks[1]
    v_packed = pl.pallas_call(
        functools.partial(pack_integrals_kernel, c_count, cap),
        out_shape=jax.ShapeDtypeStruct((IRREPS, cap * 5 // 2, LANES), jnp.bfloat16),
        in_specs=[VMEM] * 5,
        out_specs=VMEM,
        compiler_params=in_vmem(),
        name="pack_integrals",
    )(row_label[:, None], cd_label, column_slot.T, row_slot[None, :], integrals)
    v_plane = lax.all_to_all(v_packed, ("row", "sub"), 0, 0, tiled=True)
    v_all = lax.all_gather(v_plane, "plane", axis=0)

    fold = LANES // pairs
    tiles = c_total // fold
    t_slot = irrep * cap + ranks[1]
    t_packed = pl.pallas_call(
        functools.partial(pack_amplitudes_kernel, c_total, cap),
        out_shape=jax.ShapeDtypeStruct((IRREPS, tiles * cap, LANES), jnp.bfloat16),
        in_specs=[SMEM, VMEM, VMEM],
        out_specs=VMEM,
        scratch_shapes=[
            pltpu.VMEM((c_total * pairs, virtuals), jnp.bfloat16),
            pltpu.VMEM((IRREPS, cap, c_total * pairs), jnp.bfloat16),
        ],
        compiler_params=in_vmem(),
        name="pack_amplitudes",
    )(irrep[:c_total], t_slot[None, :], amplitudes)
    t_mine = lax.all_to_all(t_packed, ("row", "sub"), 0, 0, tiled=True)
    t_mine = t_mine.reshape(rows, subs, tiles, cap, fold, pairs).transpose(4, 2, 3, 0, 1, 5)
    group = rows * subs * pairs
    t_mine = t_mine.reshape(c_total * cap, group)

    lead_irrep = jnp.bitwise_xor(irrep[:c_total], mine)
    lead_spin = spin[:c_total]
    irreps = jnp.arange(IRREPS, dtype=jnp.int32)
    lows = jnp.sum(jnp.where(lead_irrep[:, None] == irreps, counts[None, :IRREPS], 0), axis=1)
    highs = jnp.sum(jnp.where(lead_irrep[:, None] == irreps, counts[None, IRREPS:], 0), axis=1)
    sums = jnp.arange(3, dtype=jnp.int32)[:, None]
    spins = sums - lead_spin[None, :]
    shift = jnp.sum(
        jnp.where(
            labels[None, None, :] == (mine + 8 * sums)[:, :, None],
            offsets.reshape(c_total, 24)[None],
            0,
        ),
        axis=2,
    )
    least = jnp.where(spins == 1, lows, 0)
    most = jnp.where(spins == 0, lows, jnp.where(spins == 1, lows + highs, 0))
    place = jnp.arange(cap, dtype=jnp.int32)
    target = jnp.where(
        (place >= least[..., None]) & (place < most[..., None]),
        place + (shift - least)[..., None],
        -1,
    ).reshape(3 * rows, c_count * cap)
    first_irrep = jnp.bitwise_xor(irrep[:a_total], mine)
    first_low = jnp.sum(
        jnp.where(first_irrep[:, None] == irreps, counts[None, :IRREPS], 0), axis=1
    )
    result = pl.pallas_call(
        functools.partial(contract_kernel, rows, subs, cap),
        out_shape=jax.ShapeDtypeStruct((rows, planes, subs, cap, group // rows), jnp.bfloat16),
        grid=(planes,),
        in_specs=[
            SMEM,
            SMEM,
            pl.BlockSpec((3 * rows, c_count * cap), lambda z: (0, 0)),
            pl.BlockSpec((c_total * cap, group), lambda z: (0, 0)),
            pl.BlockSpec((1, rows * subs, cap * 5 // 2, LANES), lambda z: (z, 0, 0, 0)),
        ],
        out_specs=pl.BlockSpec(
            (rows, 1, subs, cap, group // rows), lambda z: (0, z, 0, 0, 0)
        ),
        scratch_shapes=[
            pltpu.VMEM((3, rows * 384, group), jnp.bfloat16),
            pltpu.VMEM((cap, rows * 384), jnp.bfloat16),
        ],
        compiler_params=in_vmem(),
        name="contract",
    )(spin[:a_total], first_low, target, t_mine, v_all)
    result = result.reshape(rows * planes * subs, cap, group // rows)
    back = lax.all_to_all(result, ("row", "plane", "sub"), 0, 0, tiled=True)
    back = back.reshape(rows, planes, subs, cap, group // rows)
    spots = jnp.arange(IRREPS * cap, dtype=jnp.int32)
    rows_back = (spots[:, None] == row_slot[None, :]).astype(jnp.bfloat16)
    out = lax.dot_general(
        back,
        rows_back.reshape(rows, subs, cap, virtuals),
        (((0, 2, 3), (0, 1, 2)), ((), ())),
        preferred_element_type=jnp.float32,
    )
    return out.reshape(planes * group // rows, virtuals).astype(jnp.bfloat16)


def local(rows, planes, subs, amplitudes, integrals, irrep, spin):
    virtuals = irrep.shape[0]
    c_count = integrals.shape[1] // virtuals
    c_total = amplitudes.shape[1] // virtuals
    kind = irrep + IRREPS * spin
    hot = (kind[:, None] == jnp.arange(2 * IRREPS, dtype=jnp.int32)).astype(jnp.bfloat16)
    upto = jnp.tril(jnp.ones((virtuals, virtuals), jnp.bfloat16))
    running = jnp.dot(upto, hot, preferred_element_type=jnp.float32)
    counts = running[-1].astype(jnp.int32)
    running = running.astype(jnp.int32)
    before = jnp.concatenate([jnp.zeros((IRREPS,), jnp.int32), counts[:IRREPS]])
    here = hot > 0
    ranks = jnp.stack(
        [
            jnp.sum(jnp.where(here, running, 0), axis=1) - 1,
            jnp.sum(jnp.where(here, running + before, 0), axis=1) - 1,
        ]
    )
    labels = jnp.arange(24, dtype=jnp.int32)
    d_irrep = jnp.bitwise_xor(irrep[:c_total, None], labels % IRREPS)
    d_spin = labels // IRREPS - spin[:c_total, None]
    kinds = jnp.arange(2 * IRREPS, dtype=jnp.int32)
    found = (d_irrep[..., None] == kinds % IRREPS) & (d_spin[..., None] == kinds // IRREPS)
    sizes = jnp.sum(jnp.where(found, counts, 0), axis=2).reshape(rows, c_count, 24)
    order = jnp.arange(c_count)
    earlier = order[None, :] < order[:, None]
    offsets = jnp.sum(jnp.where(earlier[None, :, :, None], sizes[:, None], 0), axis=2)
    fits = (jnp.max(counts[:IRREPS] + counts[IRREPS:]) <= virtuals // IRREPS * 5 // 4) & (
        jnp.max(jnp.sum(sizes, axis=1)) <= c_count * virtuals // 16 * 5 // 4
    )
    return lax.cond(
        fits,
        lambda: packed(
            rows, planes, subs, amplitudes, integrals, irrep, spin, ranks, counts, offsets
        ),
        lambda: dense(amplitudes, integrals, irrep, spin),
    )


def solution(mesh):
    rows, cols = mesh.shape["row"], mesh.shape["col"]
    subs = IRREPS // rows
    planes = cols // subs
    split = Mesh(mesh.devices.reshape(rows, planes, subs), ("row", "plane", "sub"))
    col = ("plane", "sub")
    placed = (P(("row",) + col, None), P(col, "row"), P(), P())
    return jax.shard_map(
        functools.partial(local, rows, planes, subs),
        mesh=split,
        in_specs=placed,
        out_specs=P("row", col),
        check_vma=False,
    )
```

```python
import functools

import jax
import jax.numpy as jnp
from jax import lax
from jax.experimental import pallas as pl
from jax.experimental.pallas import tpu as pltpu
from jax.sharding import Mesh, PartitionSpec as P

IRREPS = 8
LANES = 128
NT = (((1,), (1,)), ((), ()))


def pair_labels(lead_irrep, lead_spin, irrep, spin):
    return jnp.bitwise_xor(lead_irrep[:, None], irrep[None, :]) + 8 * (
        lead_spin[:, None] + spin[None, :]
    )


def dense(rows, cols, amplitudes, integrals, irrep, spin):
    virtuals = irrep.shape[0]
    a_count = integrals.shape[0] // virtuals
    c_count = integrals.shape[1] // virtuals
    pairs = amplitudes.shape[0]
    col = ("plane", "sub")

    def labels(first, count):
        return pair_labels(
            lax.dynamic_slice_in_dim(irrep, first, count, 0),
            lax.dynamic_slice_in_dim(spin, first, count, 0),
            irrep,
            spin,
        ).reshape(-1)

    ab_labels = labels(lax.axis_index(col) * a_count, a_count)
    cd_labels = labels(lax.axis_index("row") * c_count, c_count)
    masked = jnp.where(
        ab_labels[:, None] == cd_labels[None, :], integrals, jnp.zeros((), integrals.dtype)
    )
    mine = lax.all_to_all(amplitudes, "row", split_axis=1, concat_axis=0, tiled=True)
    copies = jnp.broadcast_to(mine[None], (cols,) + mine.shape)
    regrouped = lax.all_to_all(copies, col, 0, 0, tiled=True)
    partial_sums = lax.dot_general(
        regrouped.reshape(-1, mine.shape[1]), masked, NT, preferred_element_type=jnp.float32
    )
    partial_sums = partial_sums.reshape(cols, rows, pairs, -1).transpose(1, 0, 2, 3)
    parts = lax.all_to_all(partial_sums, "row", 0, 0, tiled=True)
    return jnp.sum(parts, axis=0).reshape(cols * pairs, -1).astype(jnp.bfloat16)


def pack_integrals_kernel(
    c_count, c_total, subs, cap, label_cap, irrep_s, spin_s, irrep_v, spin_v, v_hbm, *refs
):
    out, slots_out, offsets_out, counts_out, fits_out, v_ref, arrived = refs
    virtuals = v_ref.shape[1]
    copies = []
    for i in range(c_count):
        copies.append(
            pltpu.make_async_copy(
                v_hbm.at[:, i * virtuals : (i + 1) * virtuals], v_ref.at[i], arrived.at[i]
            )
        )
        copies[-1].start()
    row = lax.axis_index("row")
    a = lax.axis_index("plane") * subs + lax.axis_index("sub")
    irrep, spin = irrep_v[...], spin_v[...]
    kinds = 2 * IRREPS
    kind = irrep + IRREPS * spin
    hot = lax.broadcasted_iota(jnp.int32, (kinds, virtuals), 0) == kind
    shape = (virtuals, virtuals)
    upto = lax.broadcasted_iota(jnp.int32, shape, 0) <= lax.broadcasted_iota(jnp.int32, shape, 1)
    blocks = virtuals // LANES
    shape = (LANES, LANES)
    upto = lax.broadcasted_iota(jnp.int32, shape, 0) <= lax.broadcasted_iota(jnp.int32, shape, 1)
    ones = jnp.where(hot, 1.0, 0.0)
    stacked = jnp.concatenate(
        [ones[:, k * LANES : (k + 1) * LANES] for k in range(blocks)], axis=0
    )
    inside = jnp.dot(
        stacked.astype(jnp.bfloat16),
        jnp.where(upto, 1.0, 0.0).astype(jnp.bfloat16),
        preferred_element_type=jnp.float32,
    ).astype(jnp.int32)
    counts = jnp.zeros((kinds, LANES), jnp.int32)
    running = []
    for k in range(blocks):
        block = inside[k * kinds : (k + 1) * kinds] + counts
        running.append(block)
        counts = jnp.broadcast_to(block[:, LANES - 1 :], (kinds, LANES))
    running = jnp.concatenate(running, axis=1)
    counts_out[...] = counts
    rank16 = jnp.sum(jnp.where(hot, running, 0), axis=0, keepdims=True) - 1
    before = jnp.sum(
        jnp.where(hot[IRREPS:], counts[:IRREPS, :1], 0), axis=0, keepdims=True
    )
    rank8 = rank16 + before

    which = lax.broadcasted_iota(jnp.int32, (c_total, LANES), 0)
    lead_irrep = jnp.zeros((c_total, LANES), jnp.int32)
    lead_spin = jnp.zeros((c_total, LANES), jnp.int32)
    for c in range(c_total):
        lead_irrep = jnp.where(which == c, irrep_s[c], lead_irrep)
        lead_spin = jnp.where(which == c, spin_s[c], lead_spin)
    label = lax.broadcasted_iota(jnp.int32, (c_total, LANES), 1)
    d_irrep = jnp.bitwise_xor(label & (IRREPS - 1), lead_irrep)
    d_spin = (label >> 3) - lead_spin
    d_kind = jnp.where((d_spin >= 0) & (d_spin <= 1), d_irrep + IRREPS * d_spin, -1)
    sizes = jnp.zeros((c_total, LANES), jnp.int32)
    for k in range(kinds):
        sizes = jnp.where(d_kind == k, counts[k : k + 1, :], sizes)
    within = lax.broadcasted_iota(jnp.int32, (c_total, LANES), 0) % c_count
    offsets = jnp.zeros((c_total, LANES), jnp.int32)
    for k in range(1, c_count):
        offsets += jnp.where(within >= k, pltpu.roll(sizes, k, 0), 0)
    offsets_out[...] = offsets
    irrep_most = jnp.max(counts[:IRREPS] + counts[IRREPS:])
    label_most = jnp.max(offsets + sizes)
    fits_out[0] = jnp.where((irrep_most <= cap) & (label_most <= label_cap), 1, 0)

    row_label = jnp.bitwise_xor(irrep, irrep_s[a]) + 8 * (spin + spin_s[a])
    row_slot = jnp.bitwise_xor(irrep, irrep_s[a]) * cap + rank8
    slots_out[0:1, :] = row_slot
    slots_out[1:2, :] = irrep * cap + rank8
    which = lax.broadcasted_iota(jnp.int32, (8, LANES), 0)
    first_irrep = jnp.zeros((8, LANES), jnp.int32)
    first_spin = jnp.zeros((8, LANES), jnp.int32)
    start = jnp.zeros((8, LANES), jnp.int32)
    for i in range(c_count):
        c = row * c_count + i
        first_irrep = jnp.where(which == i, irrep_s[c], first_irrep)
        first_spin = jnp.where(which == i, spin_s[c], first_spin)
        start = jnp.where(which == i, offsets_out[pl.ds(c, 1), :], start)
    cd_label = jnp.bitwise_xor(irrep, first_irrep[:, :1]) + 8 * (spin + first_spin[:, :1])
    lines = jnp.broadcast_to(rank16, (8, virtuals))
    for k in range(24):
        lines = lines + jnp.where(cd_label == k, start[:, k : k + 1], 0)
    lines = jnp.where(
        lax.broadcasted_iota(jnp.int32, (8, virtuals), 0) < c_count, lines, row_label
    )
    columns = lines.astype(jnp.float32).T.astype(jnp.int32)
    row_label = columns[:, c_count : c_count + 1]

    front = None
    for i in range(c_count):
        copies[i].wait()
        masked = jnp.where(
            row_label == cd_label[i : i + 1], v_ref[i], jnp.zeros((), v_ref.dtype)
        )
        lane = lax.broadcasted_iota(jnp.int32, (virtuals, 384), 1)
        lane = jnp.where(lane >= 320, lane - 64, lane)
        place = (columns[:, i : i + 1] == lane).astype(jnp.bfloat16)
        term = jnp.dot(masked, place, preferred_element_type=jnp.float32)
        front = term if front is None else front + term
    front = front.astype(jnp.bfloat16)
    for g in range(IRREPS):
        spot = lax.broadcasted_iota(jnp.int32, (cap, virtuals), 0) + g * cap
        rows = (row_slot == spot).astype(jnp.bfloat16)
        packed = jnp.dot(rows, front, preferred_element_type=jnp.float32)
        half = cap // 2
        left = lax.broadcasted_iota(jnp.int32, (half, LANES), 1) < 64
        tail = jnp.where(left, packed[:half, 256:], packed[half:, 256:])
        out[g, :cap, :] = packed[:, :128].astype(jnp.bfloat16)
        out[g, cap : 2 * cap, :] = packed[:, 128:256].astype(jnp.bfloat16)
        out[g, 2 * cap :, :] = tail.astype(jnp.bfloat16)


def pack_amplitudes_kernel(c_total, cap, irrep_s, slots, t_ref, out_ref, stacked, moved):
    pairs = t_ref.shape[0]
    virtuals = slots.shape[1]
    fold = LANES // pairs
    tiles = c_total // fold
    for j in range(tiles):
        for h in range(fold):
            c = h * tiles + j
            at = (j * fold + h) * pairs
            stacked[at : at + pairs, :] = t_ref[:, c * virtuals : (c + 1) * virtuals]
    for g in range(IRREPS):
        spot = lax.broadcasted_iota(jnp.int32, (cap, virtuals), 0) + g * cap
        rows = (slots[1:2, :] == spot).astype(jnp.bfloat16)
        moved[g] = lax.dot_general(
            rows, stacked[...], NT, preferred_element_type=jnp.float32
        ).astype(jnp.bfloat16)
    share = lax.broadcasted_iota(jnp.int32, (cap, LANES), 1) // pairs
    for g in range(IRREPS):
        for j in range(tiles):
            tile = None
            for h in range(fold):
                source = jnp.bitwise_xor(irrep_s[h * tiles + j], g)
                part = moved[source, :, j * LANES : (j + 1) * LANES]
                tile = part if tile is None else jnp.where(share == h, part, tile)
            out_ref[g, j * cap : (j + 1) * cap, :] = tile


def unpack_amplitudes_kernel(
    rows, subs, c_total, cap, pairs, irrep_s, spin_s, offsets, counts, t_ref, out_ref, quarter
):
    mine = lax.axis_index("row") * subs + lax.axis_index("sub")
    fold = LANES // pairs
    tiles = c_total // fold
    c_count = c_total // rows
    wide = c_count * cap
    group = out_ref.shape[2]
    main = rows * 256
    share = lax.broadcasted_iota(jnp.int32, (cap, LANES), 1) // pairs
    spot = lax.broadcasted_iota(jnp.int32, (384, wide), 0)
    spot = jnp.where(spot >= 320, spot - 64, spot)
    lane = lax.broadcasted_iota(jnp.int32, (1, wide), 1)
    for r in range(rows):
        for i in range(c_count):
            h, j = (r * c_count + i) // tiles, (r * c_count + i) % tiles
            for tile in range(group // LANES):
                whole = None
                for u in range(fold):
                    part = t_ref[tile * fold + u, j * cap : (j + 1) * cap, :]
                    if u != h:
                        part = pltpu.roll(
                            part.astype(jnp.float32), (u - h) * pairs % LANES, 1
                        ).astype(jnp.bfloat16)
                    whole = part if whole is None else jnp.where(share == u, part, whole)
                quarter[i * cap : (i + 1) * cap, tile * LANES : (tile + 1) * LANES] = whole
        for s in range(3):
            target = jnp.full((1, wide), -1, jnp.int32)
            for i in range(c_count):
                c = r * c_count + i
                irrep = jnp.bitwise_xor(irrep_s[c], mine)
                low, high = counts[irrep, 0], counts[irrep + IRREPS, 0]
                spin = s - spin_s[c]
                least = jnp.where(spin == 1, low, 0)
                most = jnp.where(spin == 0, low, jnp.where(spin == 1, low + high, 0))
                place = lane - i * cap
                inside = (place >= least) & (place < most) & (place >= 0) & (place < cap)
                start = offsets[c, mine + 8 * s]
                target = jnp.where(inside, place + (start - least), target)
            part = jnp.dot(
                (target == spot).astype(jnp.bfloat16),
                quarter[...],
                preferred_element_type=jnp.float32,
            ).astype(jnp.bfloat16)
            out_ref[s, r * 256 : (r + 1) * 256, :] = part[:256]
            out_ref[s, main + r * 128 : main + (r + 1) * 128, :] = part[256:]


def shift_of(k):
    return jnp.where(k % 2 == 1, -((k + 1) // 2), k // 2)


def contract_kernel(rows, planes, subs, first, last, irrep_s, spin_s, counts, t_ref, *refs):
    v_refs = refs[: last - first]
    if first:
        out_hbm, v_rows, sums, out_ref, copied = refs[-5:]
    else:
        out_ref, v_rows, sums = refs[-3:]
    plane = lax.axis_index("plane")
    mine = lax.axis_index("row") * subs + lax.axis_index("sub")
    n, pairs = out_ref.shape[3:]
    half = n // 2
    main = rows * 256
    left = lax.broadcasted_iota(jnp.int32, (half, LANES), 1) < 64
    for k, v_ref in enumerate(v_refs):
        for y in range(subs):
            top = y * n
            for r in range(rows):
                source = r * subs + y
                at = main + r * 128
                v_rows[k, top : top + n, r * 256 : r * 256 + 128] = v_ref[source, :n, :]
                v_rows[k, top : top + n, r * 256 + 128 : (r + 1) * 256] = v_ref[
                    source, n : 2 * n, :
                ]
                tail = v_ref[source, 2 * n :, :]
                none = jnp.zeros((), tail.dtype)
                v_rows[k, top : top + half, at : at + 128] = jnp.where(left, tail, none)
                v_rows[k, top + half : top + n, at : at + 128] = jnp.where(left, none, tail)
    slot = lax.broadcasted_iota(jnp.int32, (n, rows * pairs), 0)

    def one_plane(k, carry):
        for s in range(3):
            sums[s] = jnp.dot(v_rows[k], t_ref[s], preferred_element_type=jnp.float32)
        of = lax.rem(plane + shift_of(k + first) + planes, planes)
        for y in range(subs):
            a = of * subs + y
            s = spin_s[a]
            low = counts[jnp.bitwise_xor(irrep_s[a], mine), 0]
            lower = sums[s, y * n : (y + 1) * n, :]
            upper = sums[s + 1, y * n : (y + 1) * n, :]
            result = jnp.where(slot < low, lower, upper).astype(jnp.bfloat16)
            for r in range(rows):
                out_ref[r, k if first else of, y] = result[:, r * pairs : (r + 1) * pairs]
        return carry

    lax.fori_loop(0, last - first, one_plane, 0, unroll=last - first < 4)
    if first:
        for k in range(last - first):
            of = lax.rem(plane + shift_of(k + first) + planes, planes)
            copy = pltpu.make_async_copy(out_ref.at[:, k], out_hbm.at[:, of], copied)
            copy.start()
            copy.wait()


VMEM = pl.BlockSpec(memory_space=pltpu.VMEM)
SMEM = pl.BlockSpec(memory_space=pltpu.SMEM)
ANY = pl.BlockSpec(memory_space=pl.ANY)


def options(limit=24):
    return pltpu.CompilerParams(vmem_limit_bytes=limit * 2**20)


def cost(us):
    return pl.CostEstimate(flops=int(us * 1e9), bytes_accessed=0, transcendentals=0)


def ring_gather(block, planes):
    up = [(i, (i + 1) % planes) for i in range(planes)]
    down = [(i, (i - 1) % planes) for i in range(planes)]
    found = {0: block}
    for step in range(1, planes // 2 + 1):
        found[-step] = lax.ppermute(found[1 - step], "plane", up)
        if 2 * step < planes:
            found[step] = lax.ppermute(found[step - 1], "plane", down)
    return found


def packed(rows, planes, subs, amplitudes, irrep, spin, v_packed, slots, offsets, counts):
    virtuals = irrep.shape[0]
    pairs = amplitudes.shape[0]
    c_total = amplitudes.shape[1] // virtuals
    cap = virtuals // IRREPS * 5 // 4
    group = rows * subs * pairs
    tiles = c_total * pairs // LANES
    plane_axes, all_axes = ("row", "sub"), ("row", "plane", "sub")

    v_plane = lax.all_to_all(v_packed, plane_axes, 0, 0, tiled=True)
    found = ring_gather(v_plane, planes)
    t_packed = pl.pallas_call(
        functools.partial(pack_amplitudes_kernel, c_total, cap),
        out_shape=jax.ShapeDtypeStruct((IRREPS, tiles * cap, LANES), jnp.bfloat16),
        in_specs=[SMEM, VMEM, VMEM],
        out_specs=VMEM,
        scratch_shapes=[
            pltpu.VMEM((c_total * pairs, virtuals), jnp.bfloat16),
            pltpu.VMEM((IRREPS, cap, c_total * pairs), jnp.bfloat16),
        ],
        compiler_params=options(),
        cost_estimate=cost(8),
        name="pack_amplitudes",
    )(irrep, slots, amplitudes)
    t_mine = lax.all_to_all(t_packed, plane_axes, 0, 0, tiled=True)
    t_labels = pl.pallas_call(
        functools.partial(unpack_amplitudes_kernel, rows, subs, c_total, cap, pairs),
        out_shape=jax.ShapeDtypeStruct((3, rows * 384, group), jnp.bfloat16),
        in_specs=[SMEM] * 4 + [VMEM],
        out_specs=VMEM,
        scratch_shapes=[pltpu.VMEM((c_total // rows * cap, group), jnp.bfloat16)],
        compiler_params=options(),
        cost_estimate=cost(6),
        name="unpack_amplitudes",
    )(irrep, spin, offsets, counts, t_mine)

    shifts = sorted(found, key=abs)
    result = None
    for first, last in ((0, planes - 1), (planes - 1, planes)):
        shape = (rows, planes, subs, cap, group // rows)
        scratch = [
            pltpu.VMEM((last - first, subs * cap, rows * 384), jnp.bfloat16),
            pltpu.VMEM((3, subs * cap, group), jnp.float32),
        ]
        if first:
            scratch += [
                pltpu.VMEM((rows, last - first) + shape[2:], jnp.bfloat16),
                pltpu.SemaphoreType.DMA,
            ]
        blocks = [found[shift] for shift in shifts[first:last]]
        result = pl.pallas_call(
            functools.partial(contract_kernel, rows, planes, subs, first, last),
            out_shape=jax.ShapeDtypeStruct(shape, jnp.bfloat16),
            in_specs=[SMEM] * 3 + [VMEM] * (1 + len(blocks)) + [ANY] * bool(first),
            out_specs=ANY if first else VMEM,
            scratch_shapes=scratch,
            input_output_aliases={4 + len(blocks): 0} if first else {},
            compiler_params=options(),
            cost_estimate=cost(2 * len(blocks)),
            name="contract",
        )(irrep, spin, counts, t_labels, *blocks, *([result] if first else []))
    result = result.reshape(rows * planes * subs, cap, group // rows)
    back = lax.all_to_all(result, all_axes, 0, 0, tiled=True)
    back = back.reshape(rows, planes, subs, cap, group // rows)
    spots = jnp.arange(IRREPS * cap, dtype=jnp.int32)
    rows_back = (spots[:, None] == slots[0]).astype(jnp.bfloat16)
    out = lax.dot_general(
        back,
        rows_back.reshape(rows, subs, cap, virtuals),
        (((0, 2, 3), (0, 1, 2)), ((), ())),
        preferred_element_type=jnp.float32,
    )
    return out.reshape(planes * group // rows, virtuals).astype(jnp.bfloat16)


def local(rows, planes, subs, amplitudes, integrals, irrep, spin):
    virtuals = irrep.shape[0]
    c_count = integrals.shape[1] // virtuals
    c_total = amplitudes.shape[1] // virtuals
    cap = virtuals // IRREPS * 5 // 4
    label_cap = c_count * virtuals // (2 * IRREPS) * 5 // 4
    v_packed, slots, offsets, counts, fits = pl.pallas_call(
        functools.partial(
            pack_integrals_kernel, c_count, c_total, subs, cap, label_cap
        ),
        out_shape=[
            jax.ShapeDtypeStruct((IRREPS, cap * 5 // 2, LANES), jnp.bfloat16),
            jax.ShapeDtypeStruct((2, virtuals), jnp.int32),
            jax.ShapeDtypeStruct((c_total, LANES), jnp.int32),
            jax.ShapeDtypeStruct((2 * IRREPS, LANES), jnp.int32),
            jax.ShapeDtypeStruct((1,), jnp.int32),
        ],
        in_specs=[SMEM, SMEM, VMEM, VMEM, ANY],
        out_specs=[VMEM] * 4 + [SMEM],
        scratch_shapes=[
            pltpu.VMEM((c_count, virtuals, virtuals), jnp.bfloat16),
            pltpu.SemaphoreType.DMA((c_count,)),
        ],
        compiler_params=options(),
        cost_estimate=cost(9),
        name="pack_integrals",
    )(irrep, spin, irrep[None, :], spin[None, :], integrals)
    return lax.cond(
        fits[0] > 0,
        lambda: packed(
            rows, planes, subs, amplitudes, irrep, spin, v_packed, slots, offsets, counts
        ),
        lambda: dense(rows, planes * subs, amplitudes, integrals, irrep, spin),
    )


def solution(mesh):
    rows, cols = mesh.shape["row"], mesh.shape["col"]
    subs = IRREPS // rows
    planes = cols // subs
    split = Mesh(mesh.devices.reshape(rows, planes, subs), ("row", "plane", "sub"))
    col = ("plane", "sub")
    placed = (P(("row",) + col, None), P(col, "row"), P(), P())
    return jax.shard_map(
        functools.partial(local, rows, planes, subs),
        mesh=split,
        in_specs=placed,
        out_specs=P("row", col),
        check_vma=False,
    )
```

```python
import functools

import jax
import jax.numpy as jnp
from jax import lax
from jax.experimental import pallas as pl
from jax.experimental.pallas import tpu as pltpu
from jax.sharding import Mesh, PartitionSpec as P

IRREPS = 8
LANES = 128
NT = (((1,), (1,)), ((), ()))


def pair_labels(lead_irrep, lead_spin, irrep, spin):
    return jnp.bitwise_xor(lead_irrep[:, None], irrep[None, :]) + 8 * (
        lead_spin[:, None] + spin[None, :]
    )


def dense(rows, cols, amplitudes, integrals, irrep, spin):
    virtuals = irrep.shape[0]
    a_count = integrals.shape[0] // virtuals
    c_count = integrals.shape[1] // virtuals
    pairs = amplitudes.shape[0]
    col = ("plane", "sub")

    def labels(first, count):
        return pair_labels(
            lax.dynamic_slice_in_dim(irrep, first, count, 0),
            lax.dynamic_slice_in_dim(spin, first, count, 0),
            irrep,
            spin,
        ).reshape(-1)

    ab_labels = labels(lax.axis_index(col) * a_count, a_count)
    cd_labels = labels(lax.axis_index("row") * c_count, c_count)
    masked = jnp.where(
        ab_labels[:, None] == cd_labels[None, :], integrals, jnp.zeros((), integrals.dtype)
    )
    mine = lax.all_to_all(amplitudes, "row", split_axis=1, concat_axis=0, tiled=True)
    copies = jnp.broadcast_to(mine[None], (cols,) + mine.shape)
    regrouped = lax.all_to_all(copies, col, 0, 0, tiled=True)
    partial_sums = lax.dot_general(
        regrouped.reshape(-1, mine.shape[1]), masked, NT, preferred_element_type=jnp.float32
    )
    partial_sums = partial_sums.reshape(cols, rows, pairs, -1).transpose(1, 0, 2, 3)
    parts = lax.all_to_all(partial_sums, "row", 0, 0, tiled=True)
    return jnp.sum(parts, axis=0).reshape(cols * pairs, -1).astype(jnp.bfloat16)


def pack_integrals_kernel(
    c_count, c_total, subs, cap, label_cap, irrep_s, spin_s, irrep_v, spin_v, v_hbm, *refs
):
    out, slots_out, offsets_out, counts_out, fits_out, v_ref, arrived, ends_ref, tail_ref = refs
    virtuals = v_ref.shape[1]
    copies = []
    for i in range(c_count):
        copies.append(
            pltpu.make_async_copy(
                v_hbm.at[:, i * virtuals : (i + 1) * virtuals], v_ref.at[i], arrived.at[i]
            )
        )
        copies[-1].start()
    row = lax.axis_index("row")
    a = lax.axis_index("plane") * subs + lax.axis_index("sub")
    irrep, spin = irrep_v[...], spin_v[...]
    kinds = 2 * IRREPS
    kind = irrep + IRREPS * spin
    hot = lax.broadcasted_iota(jnp.int32, (kinds, virtuals), 0) == kind
    shape = (virtuals, virtuals)
    upto = lax.broadcasted_iota(jnp.int32, shape, 0) <= lax.broadcasted_iota(jnp.int32, shape, 1)
    blocks = virtuals // LANES
    shape = (LANES, LANES)
    upto = lax.broadcasted_iota(jnp.int32, shape, 0) <= lax.broadcasted_iota(jnp.int32, shape, 1)
    ones = jnp.where(hot, 1.0, 0.0)
    stacked = jnp.concatenate(
        [ones[:, k * LANES : (k + 1) * LANES] for k in range(blocks)], axis=0
    )
    inside = jnp.dot(
        stacked.astype(jnp.bfloat16),
        jnp.where(upto, 1.0, 0.0).astype(jnp.bfloat16),
        preferred_element_type=jnp.float32,
    ).astype(jnp.int32)
    counts = jnp.zeros((kinds, LANES), jnp.int32)
    running = []
    for k in range(blocks):
        block = inside[k * kinds : (k + 1) * kinds] + counts
        running.append(block)
        counts = jnp.broadcast_to(block[:, LANES - 1 :], (kinds, LANES))
    running = jnp.concatenate(running, axis=1)
    counts_out[...] = counts
    rank16 = jnp.sum(jnp.where(hot, running, 0), axis=0, keepdims=True) - 1
    before = jnp.sum(
        jnp.where(hot[IRREPS:], counts[:IRREPS, :1], 0), axis=0, keepdims=True
    )
    rank8 = rank16 + before

    which = lax.broadcasted_iota(jnp.int32, (c_total, LANES), 0)
    lead_irrep = jnp.zeros((c_total, LANES), jnp.int32)
    lead_spin = jnp.zeros((c_total, LANES), jnp.int32)
    for c in range(c_total):
        lead_irrep = jnp.where(which == c, irrep_s[c], lead_irrep)
        lead_spin = jnp.where(which == c, spin_s[c], lead_spin)
    label = lax.broadcasted_iota(jnp.int32, (c_total, LANES), 1)
    d_irrep = jnp.bitwise_xor(label & (IRREPS - 1), lead_irrep)
    d_spin = (label >> 3) - lead_spin
    d_kind = jnp.where((d_spin >= 0) & (d_spin <= 1), d_irrep + IRREPS * d_spin, -1)
    sizes = jnp.zeros((c_total, LANES), jnp.int32)
    for k in range(kinds):
        sizes = jnp.where(d_kind == k, counts[k : k + 1, :], sizes)
    within = lax.broadcasted_iota(jnp.int32, (c_total, LANES), 0) % c_count
    offsets = jnp.zeros((c_total, LANES), jnp.int32)
    for k in range(1, c_count):
        offsets += jnp.where(within >= k, pltpu.roll(sizes, k, 0), 0)
    ends = offsets + sizes
    offsets_out[:c_total, :] = offsets
    ends_ref[...] = ends
    over = jnp.zeros((1, LANES), jnp.int32)
    for r in range(c_total // c_count):
        offsets_out[c_total + r : c_total + r + 1, :] = over
        last = (r + 1) * c_count - 1
        over = over + jnp.maximum(ends[last : last + 1, :] - 256, 0)
    irrep_most = jnp.max(counts[:IRREPS] + counts[IRREPS:])
    fit = (irrep_most <= cap) & (jnp.max(ends) <= label_cap) & (jnp.max(over) <= LANES)
    fits_out[0] = jnp.where(fit, 1, 0)

    row_label = jnp.bitwise_xor(irrep, irrep_s[a]) + 8 * (spin + spin_s[a])
    row_slot = jnp.bitwise_xor(irrep, irrep_s[a]) * cap + rank8
    slots_out[0:1, :] = row_slot
    slots_out[1:2, :] = irrep * cap + rank8
    which = lax.broadcasted_iota(jnp.int32, (8, LANES), 0)
    first_irrep = jnp.zeros((8, LANES), jnp.int32)
    first_spin = jnp.zeros((8, LANES), jnp.int32)
    start = jnp.zeros((8, LANES), jnp.int32)
    for i in range(c_count):
        c = row * c_count + i
        first_irrep = jnp.where(which == i, irrep_s[c], first_irrep)
        first_spin = jnp.where(which == i, spin_s[c], first_spin)
        start = jnp.where(which == i, offsets_out[pl.ds(c, 1), :], start)
    cd_label = jnp.bitwise_xor(irrep, first_irrep[:, :1]) + 8 * (spin + first_spin[:, :1])
    lines = jnp.broadcast_to(rank16, (8, virtuals))
    for k in range(24):
        lines = lines + jnp.where(cd_label == k, start[:, k : k + 1], 0)
    lines = jnp.where(
        lax.broadcasted_iota(jnp.int32, (8, virtuals), 0) < c_count, lines, row_label
    )
    columns = lines.astype(jnp.float32).T.astype(jnp.int32)
    row_label = columns[:, c_count : c_count + 1]

    tail_ref[...] = jnp.zeros_like(tail_ref)
    lane = lax.broadcasted_iota(jnp.int32, (virtuals, 256), 1)
    tail_lane = 256 + lax.broadcasted_iota(jnp.int32, (virtuals, LANES), 1) % 64
    main = None
    for i in range(c_count):
        longest = jnp.max(ends_ref[pl.ds(row * c_count + i, 1), :])
        copies[i].wait()
        masked = jnp.where(
            row_label == cd_label[i : i + 1], v_ref[i], jnp.zeros((), v_ref.dtype)
        )
        slot = columns[:, i : i + 1]
        term = jnp.dot(
            masked, (slot == lane).astype(jnp.bfloat16), preferred_element_type=jnp.float32
        )
        main = term if main is None else main + term

        @pl.when(longest > 256)
        def _(masked=masked, slot=slot):
            tail_ref[...] += jnp.dot(
                masked,
                (slot == tail_lane).astype(jnp.bfloat16),
                preferred_element_type=jnp.float32,
            )

    front = jnp.concatenate([main, tail_ref[...]], axis=1).astype(jnp.bfloat16)
    for g in range(IRREPS):
        spot = lax.broadcasted_iota(jnp.int32, (cap, virtuals), 0) + g * cap
        rows = (row_slot == spot).astype(jnp.bfloat16)
        packed = jnp.dot(rows, front, preferred_element_type=jnp.float32)
        half = cap // 2
        left = lax.broadcasted_iota(jnp.int32, (half, LANES), 1) < 64
        tail = jnp.where(left, packed[:half, 256:], packed[half:, 256:])
        out[g, :cap, :] = packed[:, :128].astype(jnp.bfloat16)
        out[g, cap : 2 * cap, :] = packed[:, 128:256].astype(jnp.bfloat16)
        out[g, 2 * cap :, :] = tail.astype(jnp.bfloat16)


def pack_amplitudes_kernel(c_total, cap, irrep_s, slots, t_ref, out_ref, stacked, moved):
    pairs = t_ref.shape[0]
    virtuals = slots.shape[1]
    fold = LANES // pairs
    tiles = c_total // fold
    for j in range(tiles):
        for h in range(fold):
            c = h * tiles + j
            at = (j * fold + h) * pairs
            stacked[at : at + pairs, :] = t_ref[:, c * virtuals : (c + 1) * virtuals]
    for g in range(IRREPS):
        spot = lax.broadcasted_iota(jnp.int32, (cap, virtuals), 0) + g * cap
        rows = (slots[1:2, :] == spot).astype(jnp.bfloat16)
        moved[g] = lax.dot_general(
            rows, stacked[...], NT, preferred_element_type=jnp.float32
        ).astype(jnp.bfloat16)
    share = lax.broadcasted_iota(jnp.int32, (cap, LANES), 1) // pairs
    for g in range(IRREPS):
        for j in range(tiles):
            tile = None
            for h in range(fold):
                source = jnp.bitwise_xor(irrep_s[h * tiles + j], g)
                part = moved[source, :, j * LANES : (j + 1) * LANES]
                tile = part if tile is None else jnp.where(share == h, part, tile)
            out_ref[g, j * cap : (j + 1) * cap, :] = tile


def unpack_amplitudes_kernel(
    rows, subs, c_total, cap, pairs, irrep_s, spin_s, offsets, counts, t_ref, out_ref, quarter, tails
):
    mine = lax.axis_index("row") * subs + lax.axis_index("sub")
    fold = LANES // pairs
    tiles = c_total // fold
    c_count = c_total // rows
    wide = c_count * cap
    group = out_ref.shape[2]
    main = rows * 256
    share = lax.broadcasted_iota(jnp.int32, (cap, LANES), 1) // pairs
    spot = lax.broadcasted_iota(jnp.int32, (256 + LANES, wide), 0)
    lane = lax.broadcasted_iota(jnp.int32, (1, wide), 1)
    for r in range(rows):
        for i in range(c_count):
            h, j = (r * c_count + i) // tiles, (r * c_count + i) % tiles
            for tile in range(group // LANES):
                whole = None
                for u in range(fold):
                    part = t_ref[tile * fold + u, j * cap : (j + 1) * cap, :]
                    if u != h:
                        part = pltpu.roll(
                            part.astype(jnp.float32), (u - h) * pairs % LANES, 1
                        ).astype(jnp.bfloat16)
                    whole = part if whole is None else jnp.where(share == u, part, whole)
                quarter[i * cap : (i + 1) * cap, tile * LANES : (tile + 1) * LANES] = whole
        for s in range(3):
            target = jnp.full((1, wide), -1, jnp.int32)
            for i in range(c_count):
                c = r * c_count + i
                irrep = jnp.bitwise_xor(irrep_s[c], mine)
                low, high = counts[irrep, 0], counts[irrep + IRREPS, 0]
                spin = s - spin_s[c]
                least = jnp.where(spin == 1, low, 0)
                most = jnp.where(spin == 0, low, jnp.where(spin == 1, low + high, 0))
                place = lane - i * cap
                inside = (place >= least) & (place < most) & (place >= 0) & (place < cap)
                start = offsets[c, mine + 8 * s]
                target = jnp.where(inside, place + (start - least), target)
            over = offsets[c_total + r, mine + 8 * s]
            target = jnp.where(target >= 256, target + over, target)
            part = jnp.dot(
                (target == spot).astype(jnp.bfloat16),
                quarter[...],
                preferred_element_type=jnp.float32,
            )
            out_ref[s, r * 256 : (r + 1) * 256, :] = part[:256].astype(jnp.bfloat16)
            tails[s] = part[256:] if r == 0 else tails[s] + part[256:]
    for s in range(3):
        out_ref[s, main:, :] = tails[s].astype(jnp.bfloat16)


def join_kernel(rows, subs, cap, irrep_s, spin_s, offsets, counts, v_ref, out_ref):
    plane = lax.axis_index("plane")
    mine = lax.axis_index("row") * subs + lax.axis_index("sub")
    c_total = offsets.shape[0] - rows
    half = cap // 2
    main = 2 * cap
    for source in range(rows * subs):
        out_ref[source * main : (source + 1) * main, :] = v_ref[source, :main, :]
    left = lax.broadcasted_iota(jnp.int32, (half, LANES), 1) < 64
    place = lax.broadcasted_iota(jnp.int32, (LANES, LANES), 0) % 64
    lane = lax.broadcasted_iota(jnp.int32, (LANES, LANES), 1)
    slot = lax.broadcasted_iota(jnp.int32, (cap, LANES), 0)
    for y in range(subs):
        a = plane * subs + y
        low = counts[jnp.bitwise_xor(irrep_s[a], mine), 0]
        joined = [jnp.zeros((cap, LANES), jnp.float32) for _ in range(2)]
        for r in range(rows):
            tail = v_ref[r * subs + y, main:, :]
            none = jnp.zeros((), tail.dtype)
            wide = jnp.concatenate(
                [jnp.where(left, tail, none), jnp.where(left, none, tail)], axis=0
            )
            for k in range(2):
                over = offsets[c_total + r, mine + 8 * (spin_s[a] + k)]
                joined[k] += jnp.dot(
                    wide,
                    (place + over == lane).astype(jnp.bfloat16),
                    preferred_element_type=jnp.float32,
                )
        at = rows * subs * main + y * cap
        out_ref[at : at + cap, :] = jnp.where(slot < low, joined[0], joined[1]).astype(
            jnp.bfloat16
        )


def shift_of(k):
    return jnp.where(k % 2 == 1, -((k + 1) // 2), k // 2)


def contract_kernel(rows, planes, subs, first, last, irrep_s, spin_s, counts, t_ref, *refs):
    v_refs = refs[: last - first]
    if first:
        out_hbm, v_rows, sums, out_ref, copied = refs[-5:]
    else:
        out_ref, v_rows, sums = refs[-3:]
    plane = lax.axis_index("plane")
    mine = lax.axis_index("row") * subs + lax.axis_index("sub")
    n, pairs = out_ref.shape[3:]
    main = rows * 256
    for k, v_ref in enumerate(v_refs):
        for y in range(subs):
            top = y * n
            for r in range(rows):
                at = (r * subs + y) * 2 * n
                v_rows[k, top : top + n, r * 256 : r * 256 + 128] = v_ref[at : at + n, :]
                v_rows[k, top : top + n, r * 256 + 128 : (r + 1) * 256] = v_ref[
                    at + n : at + 2 * n, :
                ]
            at = rows * subs * 2 * n + y * n
            v_rows[k, top : top + n, main:] = v_ref[at : at + n, :]
    slot = lax.broadcasted_iota(jnp.int32, (n, rows * pairs), 0)

    def one_plane(k, carry):
        for s in range(3):
            sums[s] = jnp.dot(v_rows[k], t_ref[s], preferred_element_type=jnp.float32)
        of = lax.rem(plane + shift_of(k + first) + planes, planes)
        for y in range(subs):
            a = of * subs + y
            s = spin_s[a]
            low = counts[jnp.bitwise_xor(irrep_s[a], mine), 0]
            lower = sums[s, y * n : (y + 1) * n, :]
            upper = sums[s + 1, y * n : (y + 1) * n, :]
            result = jnp.where(slot < low, lower, upper).astype(jnp.bfloat16)
            for r in range(rows):
                out_ref[r, k if first else of, y] = result[:, r * pairs : (r + 1) * pairs]
        return carry

    lax.fori_loop(0, last - first, one_plane, 0, unroll=last - first < 4)
    if first:
        for k in range(last - first):
            of = lax.rem(plane + shift_of(k + first) + planes, planes)
            copy = pltpu.make_async_copy(out_ref.at[:, k], out_hbm.at[:, of], copied)
            copy.start()
            copy.wait()


VMEM = pl.BlockSpec(memory_space=pltpu.VMEM)
SMEM = pl.BlockSpec(memory_space=pltpu.SMEM)
ANY = pl.BlockSpec(memory_space=pl.ANY)


def options(limit=24):
    return pltpu.CompilerParams(vmem_limit_bytes=limit * 2**20)


def cost(us):
    return pl.CostEstimate(flops=int(us * 1e9), bytes_accessed=0, transcendentals=0)


def ring_gather(block, planes):
    up = [(i, (i + 1) % planes) for i in range(planes)]
    down = [(i, (i - 1) % planes) for i in range(planes)]
    found = {0: block}
    for step in range(1, planes // 2 + 1):
        found[-step] = lax.ppermute(found[1 - step], "plane", up)
        if 2 * step < planes:
            found[step] = lax.ppermute(found[step - 1], "plane", down)
    return found


def packed(rows, planes, subs, amplitudes, irrep, spin, v_packed, slots, offsets, counts):
    virtuals = irrep.shape[0]
    pairs = amplitudes.shape[0]
    c_total = amplitudes.shape[1] // virtuals
    cap = virtuals // IRREPS * 5 // 4
    group = rows * subs * pairs
    tiles = c_total * pairs // LANES
    plane_axes, all_axes = ("row", "sub"), ("row", "plane", "sub")

    v_plane = lax.all_to_all(v_packed, plane_axes, 0, 0, tiled=True)
    v_plane = pl.pallas_call(
        functools.partial(join_kernel, rows, subs, cap),
        out_shape=jax.ShapeDtypeStruct((subs * cap * (2 * rows + 1), LANES), jnp.bfloat16),
        in_specs=[SMEM] * 4 + [VMEM],
        out_specs=VMEM,
        compiler_params=options(),
        cost_estimate=cost(1.5),
        name="join_tails",
    )(irrep, spin, offsets, counts, v_plane)
    found = ring_gather(v_plane, planes)
    t_packed = pl.pallas_call(
        functools.partial(pack_amplitudes_kernel, c_total, cap),
        out_shape=jax.ShapeDtypeStruct((IRREPS, tiles * cap, LANES), jnp.bfloat16),
        in_specs=[SMEM, VMEM, VMEM],
        out_specs=VMEM,
        scratch_shapes=[
            pltpu.VMEM((c_total * pairs, virtuals), jnp.bfloat16),
            pltpu.VMEM((IRREPS, cap, c_total * pairs), jnp.bfloat16),
        ],
        compiler_params=options(),
        cost_estimate=cost(8),
        name="pack_amplitudes",
    )(irrep, slots, amplitudes)
    t_mine = lax.all_to_all(t_packed, plane_axes, 0, 0, tiled=True)
    t_labels = pl.pallas_call(
        functools.partial(unpack_amplitudes_kernel, rows, subs, c_total, cap, pairs),
        out_shape=jax.ShapeDtypeStruct((3, rows * 256 + LANES, group), jnp.bfloat16),
        in_specs=[SMEM] * 4 + [VMEM],
        out_specs=VMEM,
        scratch_shapes=[
            pltpu.VMEM((c_total // rows * cap, group), jnp.bfloat16),
            pltpu.VMEM((3, LANES, group), jnp.float32),
        ],
        compiler_params=options(),
        cost_estimate=cost(6),
        name="unpack_amplitudes",
    )(irrep, spin, offsets, counts, t_mine)

    shifts = sorted(found, key=abs)
    result = None
    for first, last in ((0, planes - 1), (planes - 1, planes)):
        shape = (rows, planes, subs, cap, group // rows)
        scratch = [
            pltpu.VMEM((last - first, subs * cap, rows * 256 + LANES), jnp.bfloat16),
            pltpu.VMEM((3, subs * cap, group), jnp.float32),
        ]
        if first:
            scratch += [
                pltpu.VMEM((rows, last - first) + shape[2:], jnp.bfloat16),
                pltpu.SemaphoreType.DMA,
            ]
        blocks = [found[shift] for shift in shifts[first:last]]
        result = pl.pallas_call(
            functools.partial(contract_kernel, rows, planes, subs, first, last),
            out_shape=jax.ShapeDtypeStruct(shape, jnp.bfloat16),
            in_specs=[SMEM] * 3 + [VMEM] * (1 + len(blocks)) + [ANY] * bool(first),
            out_specs=ANY if first else VMEM,
            scratch_shapes=scratch,
            input_output_aliases={4 + len(blocks): 0} if first else {},
            compiler_params=options(),
            cost_estimate=cost(2 * len(blocks)),
            name="contract",
        )(irrep, spin, counts, t_labels, *blocks, *([result] if first else []))
    result = result.reshape(rows * planes * subs, cap, group // rows)
    back = lax.all_to_all(result, all_axes, 0, 0, tiled=True)
    return back


def put_back(rows, planes, subs, back, slots):
    cap, group = back.shape[1], back.shape[2] * rows
    virtuals = slots.shape[1]
    back = back.reshape(rows, planes, subs, cap, group // rows)
    spots = jnp.arange(IRREPS * cap, dtype=jnp.int32)
    rows_back = (spots[:, None] == slots[0]).astype(jnp.bfloat16)
    out = lax.dot_general(
        back,
        rows_back.reshape(rows, subs, cap, virtuals),
        (((0, 2, 3), (0, 1, 2)), ((), ())),
        preferred_element_type=jnp.float32,
    )
    return out.reshape(planes * group // rows, virtuals).astype(jnp.bfloat16)


def local(rows, planes, subs, amplitudes, integrals, irrep, spin):
    virtuals = irrep.shape[0]
    c_count = integrals.shape[1] // virtuals
    c_total = amplitudes.shape[1] // virtuals
    cap = virtuals // IRREPS * 5 // 4
    label_cap = c_count * virtuals // (2 * IRREPS) * 5 // 4
    v_packed, slots, offsets, counts, fits = pl.pallas_call(
        functools.partial(
            pack_integrals_kernel, c_count, c_total, subs, cap, label_cap
        ),
        out_shape=[
            jax.ShapeDtypeStruct((IRREPS, cap * 5 // 2, LANES), jnp.bfloat16),
            jax.ShapeDtypeStruct((2, virtuals), jnp.int32),
            jax.ShapeDtypeStruct((c_total + rows, LANES), jnp.int32),
            jax.ShapeDtypeStruct((2 * IRREPS, LANES), jnp.int32),
            jax.ShapeDtypeStruct((1,), jnp.int32),
        ],
        in_specs=[SMEM, SMEM, VMEM, VMEM, ANY],
        out_specs=[VMEM] * 4 + [SMEM],
        scratch_shapes=[
            pltpu.VMEM((c_count, virtuals, virtuals), jnp.bfloat16),
            pltpu.SemaphoreType.DMA((c_count,)),
            pltpu.VMEM((c_total, LANES), jnp.int32),
            pltpu.VMEM((virtuals, LANES), jnp.float32),
        ],
        compiler_params=options(),
        cost_estimate=cost(9),
        name="pack_integrals",
    )(irrep, spin, irrep[None, :], spin[None, :], integrals)
    back = packed(rows, planes, subs, amplitudes, irrep, spin, v_packed, slots, offsets, counts)
    return lax.cond(
        fits[0] > 0,
        lambda: put_back(rows, planes, subs, back, slots),
        lambda: dense(rows, planes * subs, amplitudes, integrals, irrep, spin),
    )


def solution(mesh):
    rows, cols = mesh.shape["row"], mesh.shape["col"]
    subs = IRREPS // rows
    planes = cols // subs
    split = Mesh(mesh.devices.reshape(rows, planes, subs), ("row", "plane", "sub"))
    col = ("plane", "sub")
    placed = (P(("row",) + col, None), P(col, "row"), P(), P())
    return jax.shard_map(
        functools.partial(local, rows, planes, subs),
        mesh=split,
        in_specs=placed,
        out_specs=P("row", col),
        check_vma=False,
    )
```

```python
import functools

import jax
import jax.numpy as jnp
from jax import lax
from jax.experimental import pallas as pl
from jax.experimental.pallas import tpu as pltpu
from jax.sharding import Mesh, PartitionSpec as P

IRREPS = 8
LANES = 128
NT = (((1,), (1,)), ((), ()))


def pair_labels(lead_irrep, lead_spin, irrep, spin):
    return jnp.bitwise_xor(lead_irrep[:, None], irrep[None, :]) + 8 * (
        lead_spin[:, None] + spin[None, :]
    )


def dense(rows, cols, amplitudes, integrals, irrep, spin):
    virtuals = irrep.shape[0]
    a_count = integrals.shape[0] // virtuals
    c_count = integrals.shape[1] // virtuals
    pairs = amplitudes.shape[0]
    col = ("plane", "sub")

    def labels(first, count):
        return pair_labels(
            lax.dynamic_slice_in_dim(irrep, first, count, 0),
            lax.dynamic_slice_in_dim(spin, first, count, 0),
            irrep,
            spin,
        ).reshape(-1)

    ab_labels = labels(lax.axis_index(col) * a_count, a_count)
    cd_labels = labels(lax.axis_index("row") * c_count, c_count)
    masked = jnp.where(
        ab_labels[:, None] == cd_labels[None, :], integrals, jnp.zeros((), integrals.dtype)
    )
    mine = lax.all_to_all(amplitudes, "row", split_axis=1, concat_axis=0, tiled=True)
    copies = jnp.broadcast_to(mine[None], (cols,) + mine.shape)
    regrouped = lax.all_to_all(copies, col, 0, 0, tiled=True)
    partial_sums = lax.dot_general(
        regrouped.reshape(-1, mine.shape[1]), masked, NT, preferred_element_type=jnp.float32
    )
    partial_sums = partial_sums.reshape(cols, rows, pairs, -1).transpose(1, 0, 2, 3)
    parts = lax.all_to_all(partial_sums, "row", 0, 0, tiled=True)
    return jnp.sum(parts, axis=0).reshape(cols * pairs, -1).astype(jnp.bfloat16)


def pack_integrals_kernel(
    c_count, c_total, subs, cap, label_cap, irrep_s, spin_s, irrep_v, spin_v, v_hbm, *refs
):
    out, slots_out, offsets_out, counts_out, fits_out, v_ref, arrived, ends_ref, tail_ref = refs
    virtuals = v_ref.shape[1]
    copies = []
    for i in range(c_count):
        copies.append(
            pltpu.make_async_copy(
                v_hbm.at[:, i * virtuals : (i + 1) * virtuals], v_ref.at[i], arrived.at[i]
            )
        )
        copies[-1].start()
    row = lax.axis_index("row")
    a = lax.axis_index("plane") * subs + lax.axis_index("sub")
    irrep, spin = irrep_v[...], spin_v[...]
    kinds = 2 * IRREPS
    kind = irrep + IRREPS * spin
    hot = lax.broadcasted_iota(jnp.int32, (kinds, virtuals), 0) == kind
    shape = (virtuals, virtuals)
    upto = lax.broadcasted_iota(jnp.int32, shape, 0) <= lax.broadcasted_iota(jnp.int32, shape, 1)
    blocks = virtuals // LANES
    shape = (LANES, LANES)
    upto = lax.broadcasted_iota(jnp.int32, shape, 0) <= lax.broadcasted_iota(jnp.int32, shape, 1)
    ones = jnp.where(hot, 1.0, 0.0)
    stacked = jnp.concatenate(
        [ones[:, k * LANES : (k + 1) * LANES] for k in range(blocks)], axis=0
    )
    inside = jnp.dot(
        stacked.astype(jnp.bfloat16),
        jnp.where(upto, 1.0, 0.0).astype(jnp.bfloat16),
        preferred_element_type=jnp.float32,
    ).astype(jnp.int32)
    counts = jnp.zeros((kinds, LANES), jnp.int32)
    running = []
    for k in range(blocks):
        block = inside[k * kinds : (k + 1) * kinds] + counts
        running.append(block)
        counts = jnp.broadcast_to(block[:, LANES - 1 :], (kinds, LANES))
    running = jnp.concatenate(running, axis=1)
    counts_out[...] = counts
    rank16 = jnp.sum(jnp.where(hot, running, 0), axis=0, keepdims=True) - 1
    before = jnp.sum(
        jnp.where(hot[IRREPS:], counts[:IRREPS, :1], 0), axis=0, keepdims=True
    )
    rank8 = rank16 + before

    which = lax.broadcasted_iota(jnp.int32, (c_total, LANES), 0)
    lead_irrep = jnp.zeros((c_total, LANES), jnp.int32)
    lead_spin = jnp.zeros((c_total, LANES), jnp.int32)
    for c in range(c_total):
        lead_irrep = jnp.where(which == c, irrep_s[c], lead_irrep)
        lead_spin = jnp.where(which == c, spin_s[c], lead_spin)
    label = lax.broadcasted_iota(jnp.int32, (c_total, LANES), 1)
    d_irrep = jnp.bitwise_xor(label & (IRREPS - 1), lead_irrep)
    d_spin = (label >> 3) - lead_spin
    d_kind = jnp.where((d_spin >= 0) & (d_spin <= 1), d_irrep + IRREPS * d_spin, -1)
    sizes = jnp.zeros((c_total, LANES), jnp.int32)
    for k in range(kinds):
        sizes = jnp.where(d_kind == k, counts[k : k + 1, :], sizes)
    within = lax.broadcasted_iota(jnp.int32, (c_total, LANES), 0) % c_count
    offsets = jnp.zeros((c_total, LANES), jnp.int32)
    for k in range(1, c_count):
        offsets += jnp.where(within >= k, pltpu.roll(sizes, k, 0), 0)
    ends = offsets + sizes
    offsets_out[:c_total, :] = offsets
    ends_ref[...] = ends
    over = jnp.zeros((1, LANES), jnp.int32)
    for r in range(c_total // c_count):
        offsets_out[c_total + r : c_total + r + 1, :] = over
        last = (r + 1) * c_count - 1
        over = over + jnp.maximum(ends[last : last + 1, :] - 256, 0)
    irrep_most = jnp.max(counts[:IRREPS] + counts[IRREPS:])
    fit = (irrep_most <= cap) & (jnp.max(ends) <= label_cap) & (jnp.max(over) <= LANES)
    fits_out[0] = jnp.where(fit, 1, 0)

    row_label = jnp.bitwise_xor(irrep, irrep_s[a]) + 8 * (spin + spin_s[a])
    row_slot = jnp.bitwise_xor(irrep, irrep_s[a]) * cap + rank8
    slots_out[0:1, :] = row_slot
    slots_out[1:2, :] = irrep * cap + rank8
    which = lax.broadcasted_iota(jnp.int32, (8, LANES), 0)
    first_irrep = jnp.zeros((8, LANES), jnp.int32)
    first_spin = jnp.zeros((8, LANES), jnp.int32)
    start = jnp.zeros((8, LANES), jnp.int32)
    for i in range(c_count):
        c = row * c_count + i
        first_irrep = jnp.where(which == i, irrep_s[c], first_irrep)
        first_spin = jnp.where(which == i, spin_s[c], first_spin)
        start = jnp.where(which == i, offsets_out[pl.ds(c, 1), :], start)
    cd_label = jnp.bitwise_xor(irrep, first_irrep[:, :1]) + 8 * (spin + first_spin[:, :1])
    lines = jnp.broadcast_to(rank16, (8, virtuals))
    for k in range(24):
        lines = lines + jnp.where(cd_label == k, start[:, k : k + 1], 0)
    lines = jnp.where(
        lax.broadcasted_iota(jnp.int32, (8, virtuals), 0) < c_count, lines, row_label
    )
    columns = lines.astype(jnp.float32).T.astype(jnp.int32)
    row_label = columns[:, c_count : c_count + 1]

    tail_ref[...] = jnp.zeros_like(tail_ref)
    lane = lax.broadcasted_iota(jnp.int32, (virtuals, 256), 1)
    tail_lane = 256 + lax.broadcasted_iota(jnp.int32, (virtuals, LANES), 1) % 64
    main = None
    for i in range(c_count):
        longest = jnp.max(ends_ref[pl.ds(row * c_count + i, 1), :])
        copies[i].wait()
        masked = jnp.where(
            row_label == cd_label[i : i + 1], v_ref[i], jnp.zeros((), v_ref.dtype)
        )
        slot = columns[:, i : i + 1]
        term = jnp.dot(
            masked, (slot == lane).astype(jnp.bfloat16), preferred_element_type=jnp.float32
        )
        main = term if main is None else main + term

        @pl.when(longest > 256)
        def _(masked=masked, slot=slot):
            tail_ref[...] += jnp.dot(
                masked,
                (slot == tail_lane).astype(jnp.bfloat16),
                preferred_element_type=jnp.float32,
            )

    front = jnp.concatenate([main, tail_ref[...]], axis=1).astype(jnp.bfloat16)
    for g in range(IRREPS):
        spot = lax.broadcasted_iota(jnp.int32, (cap, virtuals), 0) + g * cap
        rows = (row_slot == spot).astype(jnp.bfloat16)
        packed = jnp.dot(rows, front, preferred_element_type=jnp.float32)
        half = cap // 2
        left = lax.broadcasted_iota(jnp.int32, (half, LANES), 1) < 64
        tail = jnp.where(left, packed[:half, 256:], packed[half:, 256:])
        out[g, :cap, :] = packed[:, :128].astype(jnp.bfloat16)
        out[g, cap : 2 * cap, :] = packed[:, 128:256].astype(jnp.bfloat16)
        out[g, 2 * cap :, :] = tail.astype(jnp.bfloat16)


def pack_amplitudes_kernel(c_total, cap, irrep_s, slots, t_ref, out_ref, stacked, moved):
    pairs = t_ref.shape[0]
    virtuals = slots.shape[1]
    fold = LANES // pairs
    tiles = c_total // fold
    for j in range(tiles):
        for h in range(fold):
            c = h * tiles + j
            at = (j * fold + h) * pairs
            stacked[at : at + pairs, :] = t_ref[:, c * virtuals : (c + 1) * virtuals]
    for g in range(IRREPS):
        spot = lax.broadcasted_iota(jnp.int32, (cap, virtuals), 0) + g * cap
        rows = (slots[1:2, :] == spot).astype(jnp.bfloat16)
        moved[g] = lax.dot_general(
            rows, stacked[...], NT, preferred_element_type=jnp.float32
        ).astype(jnp.bfloat16)
    share = lax.broadcasted_iota(jnp.int32, (cap, LANES), 1) // pairs
    for g in range(IRREPS):
        for j in range(tiles):
            tile = None
            for h in range(fold):
                source = jnp.bitwise_xor(irrep_s[h * tiles + j], g)
                part = moved[source, :, j * LANES : (j + 1) * LANES]
                tile = part if tile is None else jnp.where(share == h, part, tile)
            out_ref[g, j * cap : (j + 1) * cap, :] = tile


def unpack_amplitudes_kernel(
    rows, subs, c_total, cap, pairs, irrep_s, spin_s, offsets, counts, t_ref, out_ref, quarter, tails
):
    mine = lax.axis_index("row") * subs + lax.axis_index("sub")
    fold = LANES // pairs
    tiles = c_total // fold
    c_count = c_total // rows
    wide = c_count * cap
    group = out_ref.shape[2]
    main = rows * 256
    share = lax.broadcasted_iota(jnp.int32, (cap, LANES), 1) // pairs
    spot = lax.broadcasted_iota(jnp.int32, (256 + LANES, wide), 0)
    lane = lax.broadcasted_iota(jnp.int32, (1, wide), 1)
    for r in range(rows):
        for i in range(c_count):
            h, j = (r * c_count + i) // tiles, (r * c_count + i) % tiles
            for tile in range(group // LANES):
                whole = None
                for u in range(fold):
                    part = t_ref[tile * fold + u, j * cap : (j + 1) * cap, :]
                    if u != h:
                        part = pltpu.roll(
                            part.astype(jnp.float32), (u - h) * pairs % LANES, 1
                        ).astype(jnp.bfloat16)
                    whole = part if whole is None else jnp.where(share == u, part, whole)
                quarter[i * cap : (i + 1) * cap, tile * LANES : (tile + 1) * LANES] = whole
        for s in range(3):
            target = jnp.full((1, wide), -1, jnp.int32)
            for i in range(c_count):
                c = r * c_count + i
                irrep = jnp.bitwise_xor(irrep_s[c], mine)
                low, high = counts[irrep, 0], counts[irrep + IRREPS, 0]
                spin = s - spin_s[c]
                least = jnp.where(spin == 1, low, 0)
                most = jnp.where(spin == 0, low, jnp.where(spin == 1, low + high, 0))
                place = lane - i * cap
                inside = (place >= least) & (place < most) & (place >= 0) & (place < cap)
                start = offsets[c, mine + 8 * s]
                target = jnp.where(inside, place + (start - least), target)
            over = offsets[c_total + r, mine + 8 * s]
            target = jnp.where(target >= 256, target + over, target)
            part = jnp.dot(
                (target == spot).astype(jnp.bfloat16),
                quarter[...],
                preferred_element_type=jnp.float32,
            )
            out_ref[s, r * 256 : (r + 1) * 256, :] = part[:256].astype(jnp.bfloat16)
            tails[s] = part[256:] if r == 0 else tails[s] + part[256:]
    for s in range(3):
        out_ref[s, main:, :] = tails[s].astype(jnp.bfloat16)


def join_kernel(rows, subs, cap, irrep_s, spin_s, offsets, counts, v_ref, out_ref):
    plane = lax.axis_index("plane")
    mine = lax.axis_index("row") * subs + lax.axis_index("sub")
    c_total = offsets.shape[0] - rows
    half = cap // 2
    main = 2 * cap
    for source in range(rows * subs):
        out_ref[source * main : (source + 1) * main, :] = v_ref[source, :main, :]
    left = lax.broadcasted_iota(jnp.int32, (half, LANES), 1) < 64
    place = lax.broadcasted_iota(jnp.int32, (LANES, LANES), 0) % 64
    lane = lax.broadcasted_iota(jnp.int32, (LANES, LANES), 1)
    slot = lax.broadcasted_iota(jnp.int32, (cap, LANES), 0)
    for y in range(subs):
        a = plane * subs + y
        low = counts[jnp.bitwise_xor(irrep_s[a], mine), 0]
        joined = [jnp.zeros((cap, LANES), jnp.float32) for _ in range(2)]
        for r in range(rows):
            tail = v_ref[r * subs + y, main:, :]
            none = jnp.zeros((), tail.dtype)
            wide = jnp.concatenate(
                [jnp.where(left, tail, none), jnp.where(left, none, tail)], axis=0
            )
            for k in range(2):
                over = offsets[c_total + r, mine + 8 * (spin_s[a] + k)]
                joined[k] += jnp.dot(
                    wide,
                    (place + over == lane).astype(jnp.bfloat16),
                    preferred_element_type=jnp.float32,
                )
        at = rows * subs * main + y * cap
        out_ref[at : at + cap, :] = jnp.where(slot < low, joined[0], joined[1]).astype(
            jnp.bfloat16
        )


def shift_of(k):
    return jnp.where(k % 2 == 1, -((k + 1) // 2), k // 2)


def contract_kernel(rows, planes, subs, first, last, irrep_s, spin_s, counts, t_ref, *refs):
    v_refs = refs[: last - first]
    if first:
        out_hbm, v_rows, out_ref, copied = refs[-4:]
    else:
        out_ref, v_rows = refs[-2:]
    plane = lax.axis_index("plane")
    mine = lax.axis_index("row") * subs + lax.axis_index("sub")
    n, pairs = out_ref.shape[3:]
    main = rows * 256
    for k, v_ref in enumerate(v_refs):
        for y in range(subs):
            top = y * n
            for r in range(rows):
                at = (r * subs + y) * 2 * n
                v_rows[k, top : top + n, r * 256 : r * 256 + 128] = v_ref[at : at + n, :]
                v_rows[k, top : top + n, r * 256 + 128 : (r + 1) * 256] = v_ref[
                    at + n : at + 2 * n, :
                ]
            at = rows * subs * 2 * n + y * n
            v_rows[k, top : top + n, main:] = v_ref[at : at + n, :]
    slot = lax.broadcasted_iota(jnp.int32, (n, rows * pairs), 0)

    def one_plane(k, carry):
        of = lax.rem(plane + shift_of(k + first) + planes, planes)
        for y in range(subs):
            a = of * subs + y
            s = spin_s[a]
            low = counts[jnp.bitwise_xor(irrep_s[a], mine), 0]
            block = v_rows[k, y * n : (y + 1) * n, :]
            lower = jnp.dot(block, t_ref[s], preferred_element_type=jnp.float32)
            upper = jnp.dot(block, t_ref[s + 1], preferred_element_type=jnp.float32)
            result = jnp.where(slot < low, lower, upper).astype(jnp.bfloat16)
            for r in range(rows):
                out_ref[r, k if first else of, y] = result[:, r * pairs : (r + 1) * pairs]
        return carry

    lax.fori_loop(0, last - first, one_plane, 0, unroll=last - first < 4)
    if first:
        for k in range(last - first):
            of = lax.rem(plane + shift_of(k + first) + planes, planes)
            copy = pltpu.make_async_copy(out_ref.at[:, k], out_hbm.at[:, of], copied)
            copy.start()
            copy.wait()


VMEM = pl.BlockSpec(memory_space=pltpu.VMEM)
SMEM = pl.BlockSpec(memory_space=pltpu.SMEM)
ANY = pl.BlockSpec(memory_space=pl.ANY)


def options(limit=24):
    return pltpu.CompilerParams(vmem_limit_bytes=limit * 2**20)


def cost(us):
    return pl.CostEstimate(flops=int(us * 1e9), bytes_accessed=0, transcendentals=0)


def ring_gather(block, planes):
    up = [(i, (i + 1) % planes) for i in range(planes)]
    down = [(i, (i - 1) % planes) for i in range(planes)]
    found = {0: block}
    for step in range(1, planes // 2 + 1):
        found[-step] = lax.ppermute(found[1 - step], "plane", up)
        if 2 * step < planes:
            found[step] = lax.ppermute(found[step - 1], "plane", down)
    return found


def packed(rows, planes, subs, amplitudes, irrep, spin, v_packed, slots, offsets, counts):
    virtuals = irrep.shape[0]
    pairs = amplitudes.shape[0]
    c_total = amplitudes.shape[1] // virtuals
    cap = virtuals // IRREPS * 5 // 4
    group = rows * subs * pairs
    tiles = c_total * pairs // LANES
    plane_axes, all_axes = ("row", "sub"), ("row", "plane", "sub")

    v_plane = lax.all_to_all(v_packed, plane_axes, 0, 0, tiled=True)
    v_plane = pl.pallas_call(
        functools.partial(join_kernel, rows, subs, cap),
        out_shape=jax.ShapeDtypeStruct((subs * cap * (2 * rows + 1), LANES), jnp.bfloat16),
        in_specs=[SMEM] * 4 + [VMEM],
        out_specs=VMEM,
        compiler_params=options(),
        cost_estimate=cost(1.5),
        name="join_tails",
    )(irrep, spin, offsets, counts, v_plane)
    found = ring_gather(v_plane, planes)
    t_packed = pl.pallas_call(
        functools.partial(pack_amplitudes_kernel, c_total, cap),
        out_shape=jax.ShapeDtypeStruct((IRREPS, tiles * cap, LANES), jnp.bfloat16),
        in_specs=[SMEM, VMEM, VMEM],
        out_specs=VMEM,
        scratch_shapes=[
            pltpu.VMEM((c_total * pairs, virtuals), jnp.bfloat16),
            pltpu.VMEM((IRREPS, cap, c_total * pairs), jnp.bfloat16),
        ],
        compiler_params=options(),
        cost_estimate=cost(8),
        name="pack_amplitudes",
    )(irrep, slots, amplitudes)
    t_mine = lax.all_to_all(t_packed, plane_axes, 0, 0, tiled=True)
    t_labels = pl.pallas_call(
        functools.partial(unpack_amplitudes_kernel, rows, subs, c_total, cap, pairs),
        out_shape=jax.ShapeDtypeStruct((3, rows * 256 + LANES, group), jnp.bfloat16),
        in_specs=[SMEM] * 4 + [VMEM],
        out_specs=VMEM,
        scratch_shapes=[
            pltpu.VMEM((c_total // rows * cap, group), jnp.bfloat16),
            pltpu.VMEM((3, LANES, group), jnp.float32),
        ],
        compiler_params=options(),
        cost_estimate=cost(6),
        name="unpack_amplitudes",
    )(irrep, spin, offsets, counts, t_mine)

    shifts = sorted(found, key=abs)
    result = None
    for first, last in ((0, planes - 1), (planes - 1, planes)):
        shape = (rows, planes, subs, cap, group // rows)
        scratch = [
            pltpu.VMEM((last - first, subs * cap, rows * 256 + LANES), jnp.bfloat16),
        ]
        if first:
            scratch += [
                pltpu.VMEM((rows, last - first) + shape[2:], jnp.bfloat16),
                pltpu.SemaphoreType.DMA,
            ]
        blocks = [found[shift] for shift in shifts[first:last]]
        result = pl.pallas_call(
            functools.partial(contract_kernel, rows, planes, subs, first, last),
            out_shape=jax.ShapeDtypeStruct(shape, jnp.bfloat16),
            in_specs=[SMEM] * 3 + [VMEM] * (1 + len(blocks)) + [ANY] * bool(first),
            out_specs=ANY if first else VMEM,
            scratch_shapes=scratch,
            input_output_aliases={4 + len(blocks): 0} if first else {},
            compiler_params=options(),
            cost_estimate=cost(2 * len(blocks)),
            name="contract",
        )(irrep, spin, counts, t_labels, *blocks, *([result] if first else []))
    result = result.reshape(rows * planes * subs, cap, group // rows)
    back = lax.all_to_all(result, all_axes, 0, 0, tiled=True)
    return back


def put_back(rows, planes, subs, back, slots):
    cap, group = back.shape[1], back.shape[2] * rows
    virtuals = slots.shape[1]
    back = back.reshape(rows, planes, subs, cap, group // rows)
    spots = jnp.arange(IRREPS * cap, dtype=jnp.int32)
    rows_back = (spots[:, None] == slots[0]).astype(jnp.bfloat16)
    out = lax.dot_general(
        back,
        rows_back.reshape(rows, subs, cap, virtuals),
        (((0, 2, 3), (0, 1, 2)), ((), ())),
        preferred_element_type=jnp.float32,
    )
    return out.reshape(planes * group // rows, virtuals).astype(jnp.bfloat16)


def local(rows, planes, subs, amplitudes, integrals, irrep, spin):
    virtuals = irrep.shape[0]
    c_count = integrals.shape[1] // virtuals
    c_total = amplitudes.shape[1] // virtuals
    cap = virtuals // IRREPS * 5 // 4
    label_cap = c_count * virtuals // (2 * IRREPS) * 5 // 4
    v_packed, slots, offsets, counts, fits = pl.pallas_call(
        functools.partial(
            pack_integrals_kernel, c_count, c_total, subs, cap, label_cap
        ),
        out_shape=[
            jax.ShapeDtypeStruct((IRREPS, cap * 5 // 2, LANES), jnp.bfloat16),
            jax.ShapeDtypeStruct((2, virtuals), jnp.int32),
            jax.ShapeDtypeStruct((c_total + rows, LANES), jnp.int32),
            jax.ShapeDtypeStruct((2 * IRREPS, LANES), jnp.int32),
            jax.ShapeDtypeStruct((1,), jnp.int32),
        ],
        in_specs=[SMEM, SMEM, VMEM, VMEM, ANY],
        out_specs=[VMEM] * 4 + [SMEM],
        scratch_shapes=[
            pltpu.VMEM((c_count, virtuals, virtuals), jnp.bfloat16),
            pltpu.SemaphoreType.DMA((c_count,)),
            pltpu.VMEM((c_total, LANES), jnp.int32),
            pltpu.VMEM((virtuals, LANES), jnp.float32),
        ],
        compiler_params=options(),
        cost_estimate=cost(9),
        name="pack_integrals",
    )(irrep, spin, irrep[None, :], spin[None, :], integrals)
    back = packed(rows, planes, subs, amplitudes, irrep, spin, v_packed, slots, offsets, counts)
    return lax.cond(
        fits[0] > 0,
        lambda: put_back(rows, planes, subs, back, slots),
        lambda: dense(rows, planes * subs, amplitudes, integrals, irrep, spin),
    )


def solution(mesh):
    rows, cols = mesh.shape["row"], mesh.shape["col"]
    subs = IRREPS // rows
    planes = cols // subs
    split = Mesh(mesh.devices.reshape(rows, planes, subs), ("row", "plane", "sub"))
    col = ("plane", "sub")
    placed = (P(("row",) + col, None), P(col, "row"), P(), P())
    return jax.shard_map(
        functools.partial(local, rows, planes, subs),
        mesh=split,
        in_specs=placed,
        out_specs=P("row", col),
        check_vma=False,
    )
```

```python
import functools

import jax
import jax.numpy as jnp
from jax import lax
from jax.experimental import pallas as pl
from jax.experimental.pallas import tpu as pltpu
from jax.sharding import Mesh, PartitionSpec as P

IRREPS = 8
LANES = 128
NT = (((1,), (1,)), ((), ()))


def pair_labels(lead_irrep, lead_spin, irrep, spin):
    return jnp.bitwise_xor(lead_irrep[:, None], irrep[None, :]) + 8 * (
        lead_spin[:, None] + spin[None, :]
    )


def dense(rows, cols, amplitudes, integrals, irrep, spin):
    virtuals = irrep.shape[0]
    a_count = integrals.shape[0] // virtuals
    c_count = integrals.shape[1] // virtuals
    pairs = amplitudes.shape[0]
    col = ("plane", "sub")

    def labels(first, count):
        return pair_labels(
            lax.dynamic_slice_in_dim(irrep, first, count, 0),
            lax.dynamic_slice_in_dim(spin, first, count, 0),
            irrep,
            spin,
        ).reshape(-1)

    ab_labels = labels(lax.axis_index(col) * a_count, a_count)
    cd_labels = labels(lax.axis_index("row") * c_count, c_count)
    masked = jnp.where(
        ab_labels[:, None] == cd_labels[None, :], integrals, jnp.zeros((), integrals.dtype)
    )
    mine = lax.all_to_all(amplitudes, "row", split_axis=1, concat_axis=0, tiled=True)
    copies = jnp.broadcast_to(mine[None], (cols,) + mine.shape)
    regrouped = lax.all_to_all(copies, col, 0, 0, tiled=True)
    partial_sums = lax.dot_general(
        regrouped.reshape(-1, mine.shape[1]), masked, NT, preferred_element_type=jnp.float32
    )
    partial_sums = partial_sums.reshape(cols, rows, pairs, -1).transpose(1, 0, 2, 3)
    parts = lax.all_to_all(partial_sums, "row", 0, 0, tiled=True)
    return jnp.sum(parts, axis=0).reshape(cols * pairs, -1).astype(jnp.bfloat16)


def pack_integrals_kernel(
    c_count, c_total, subs, cap, label_cap, irrep_s, spin_s, irrep_v, spin_v, v_hbm, *refs
):
    out, slots_out, offsets_out, counts_out, fits_out, v_ref, arrived, ends_ref, tail_ref = refs
    virtuals = v_ref.shape[1]
    copies = []
    for i in range(c_count):
        copies.append(
            pltpu.make_async_copy(
                v_hbm.at[:, i * virtuals : (i + 1) * virtuals], v_ref.at[i], arrived.at[i]
            )
        )
        copies[-1].start()
    row = lax.axis_index("row")
    a = lax.axis_index("plane") * subs + lax.axis_index("sub")
    irrep, spin = irrep_v[...], spin_v[...]
    kinds = 2 * IRREPS
    kind = irrep + IRREPS * spin
    hot = lax.broadcasted_iota(jnp.int32, (kinds, virtuals), 0) == kind
    shape = (virtuals, virtuals)
    upto = lax.broadcasted_iota(jnp.int32, shape, 0) <= lax.broadcasted_iota(jnp.int32, shape, 1)
    blocks = virtuals // LANES
    shape = (LANES, LANES)
    upto = lax.broadcasted_iota(jnp.int32, shape, 0) <= lax.broadcasted_iota(jnp.int32, shape, 1)
    ones = jnp.where(hot, 1.0, 0.0)
    stacked = jnp.concatenate(
        [ones[:, k * LANES : (k + 1) * LANES] for k in range(blocks)], axis=0
    )
    inside = jnp.dot(
        stacked.astype(jnp.bfloat16),
        jnp.where(upto, 1.0, 0.0).astype(jnp.bfloat16),
        preferred_element_type=jnp.float32,
    ).astype(jnp.int32)
    counts = jnp.zeros((kinds, LANES), jnp.int32)
    running = []
    for k in range(blocks):
        block = inside[k * kinds : (k + 1) * kinds] + counts
        running.append(block)
        counts = jnp.broadcast_to(block[:, LANES - 1 :], (kinds, LANES))
    running = jnp.concatenate(running, axis=1)
    counts_out[...] = counts
    rank16 = jnp.sum(jnp.where(hot, running, 0), axis=0, keepdims=True) - 1
    before = jnp.sum(
        jnp.where(hot[IRREPS:], counts[:IRREPS, :1], 0), axis=0, keepdims=True
    )
    rank8 = rank16 + before

    which = lax.broadcasted_iota(jnp.int32, (c_total, LANES), 0)
    lead_irrep = jnp.zeros((c_total, LANES), jnp.int32)
    lead_spin = jnp.zeros((c_total, LANES), jnp.int32)
    for c in range(c_total):
        lead_irrep = jnp.where(which == c, irrep_s[c], lead_irrep)
        lead_spin = jnp.where(which == c, spin_s[c], lead_spin)
    label = lax.broadcasted_iota(jnp.int32, (c_total, LANES), 1)
    d_irrep = jnp.bitwise_xor(label & (IRREPS - 1), lead_irrep)
    d_spin = (label >> 3) - lead_spin
    d_kind = jnp.where((d_spin >= 0) & (d_spin <= 1), d_irrep + IRREPS * d_spin, -1)
    sizes = jnp.zeros((c_total, LANES), jnp.int32)
    for k in range(kinds):
        sizes = jnp.where(d_kind == k, counts[k : k + 1, :], sizes)
    within = lax.broadcasted_iota(jnp.int32, (c_total, LANES), 0) % c_count
    offsets = jnp.zeros((c_total, LANES), jnp.int32)
    for k in range(1, c_count):
        offsets += jnp.where(within >= k, pltpu.roll(sizes, k, 0), 0)
    ends = offsets + sizes
    offsets_out[:c_total, :] = offsets
    ends_ref[...] = ends
    over = jnp.zeros((1, LANES), jnp.int32)
    for r in range(c_total // c_count):
        offsets_out[c_total + r : c_total + r + 1, :] = over
        last = (r + 1) * c_count - 1
        over = over + jnp.maximum(ends[last : last + 1, :] - 256, 0)
    irrep_most = jnp.max(counts[:IRREPS] + counts[IRREPS:])
    fit = (irrep_most <= cap) & (jnp.max(ends) <= label_cap) & (jnp.max(over) <= LANES)
    fits_out[0] = jnp.where(fit, 1, 0)

    row_label = jnp.bitwise_xor(irrep, irrep_s[a]) + 8 * (spin + spin_s[a])
    row_slot = jnp.bitwise_xor(irrep, irrep_s[a]) * cap + rank8
    slots_out[0:1, :] = row_slot
    slots_out[1:2, :] = irrep * cap + rank8
    which = lax.broadcasted_iota(jnp.int32, (8, LANES), 0)
    first_irrep = jnp.zeros((8, LANES), jnp.int32)
    first_spin = jnp.zeros((8, LANES), jnp.int32)
    start = jnp.zeros((8, LANES), jnp.int32)
    for i in range(c_count):
        c = row * c_count + i
        first_irrep = jnp.where(which == i, irrep_s[c], first_irrep)
        first_spin = jnp.where(which == i, spin_s[c], first_spin)
        start = jnp.where(which == i, offsets_out[pl.ds(c, 1), :], start)
    cd_label = jnp.bitwise_xor(irrep, first_irrep[:, :1]) + 8 * (spin + first_spin[:, :1])
    lines = jnp.broadcast_to(rank16, (8, virtuals))
    for k in range(24):
        lines = lines + jnp.where(cd_label == k, start[:, k : k + 1], 0)
    lines = jnp.where(
        lax.broadcasted_iota(jnp.int32, (8, virtuals), 0) < c_count, lines, row_label
    )
    columns = lines.astype(jnp.float32).T.astype(jnp.int32)
    row_label = columns[:, c_count : c_count + 1]

    tail_ref[...] = jnp.zeros_like(tail_ref)
    lane = lax.broadcasted_iota(jnp.int32, (virtuals, 256), 1)
    tail_lane = 256 + lax.broadcasted_iota(jnp.int32, (virtuals, LANES), 1) % 64
    longest = [jnp.max(ends_ref[pl.ds(row * c_count + i, 1), :]) for i in range(c_count)]
    main = None
    for i in range(c_count):
        copies[i].wait()
        masked = jnp.where(
            row_label == cd_label[i : i + 1], v_ref[i], jnp.zeros((), v_ref.dtype)
        )
        slot = columns[:, i : i + 1]
        term = jnp.dot(
            masked, (slot == lane).astype(jnp.bfloat16), preferred_element_type=jnp.float32
        )
        main = term if main is None else main + term

        @pl.when(longest[i] > 256)
        def _(masked=masked, slot=slot):
            tail_ref[...] += jnp.dot(
                masked,
                (slot == tail_lane).astype(jnp.bfloat16),
                preferred_element_type=jnp.float32,
            )

    front = jnp.concatenate([main, tail_ref[...]], axis=1).astype(jnp.bfloat16)
    for g in range(IRREPS):
        spot = lax.broadcasted_iota(jnp.int32, (cap, virtuals), 0) + g * cap
        rows = (row_slot == spot).astype(jnp.bfloat16)
        packed = jnp.dot(rows, front, preferred_element_type=jnp.float32)
        half = cap // 2
        left = lax.broadcasted_iota(jnp.int32, (half, LANES), 1) < 64
        tail = jnp.where(left, packed[:half, 256:], packed[half:, 256:])
        out[g, :cap, :] = packed[:, :128].astype(jnp.bfloat16)
        out[g, cap : 2 * cap, :] = packed[:, 128:256].astype(jnp.bfloat16)
        out[g, 2 * cap :, :] = tail.astype(jnp.bfloat16)


def pack_amplitudes_kernel(c_total, cap, irrep_s, slots, t_ref, out_ref, stacked, moved):
    pairs = t_ref.shape[0]
    virtuals = slots.shape[1]
    fold = LANES // pairs
    tiles = c_total // fold
    for j in range(tiles):
        for h in range(fold):
            c = h * tiles + j
            at = (j * fold + h) * pairs
            stacked[at : at + pairs, :] = t_ref[:, c * virtuals : (c + 1) * virtuals]
    for g in range(IRREPS):
        spot = lax.broadcasted_iota(jnp.int32, (cap, virtuals), 0) + g * cap
        rows = (slots[1:2, :] == spot).astype(jnp.bfloat16)
        moved[g] = lax.dot_general(
            rows, stacked[...], NT, preferred_element_type=jnp.float32
        ).astype(jnp.bfloat16)
    share = lax.broadcasted_iota(jnp.int32, (cap, LANES), 1) // pairs
    for g in range(IRREPS):
        for j in range(tiles):
            tile = None
            for h in range(fold):
                source = jnp.bitwise_xor(irrep_s[h * tiles + j], g)
                part = moved[source, :, j * LANES : (j + 1) * LANES]
                tile = part if tile is None else jnp.where(share == h, part, tile)
            out_ref[g, j * cap : (j + 1) * cap, :] = tile


def unpack_amplitudes_kernel(
    rows, subs, c_total, cap, pairs, irrep_s, spin_s, offsets, counts, t_ref, out_ref, quarter, tails
):
    mine = lax.axis_index("row") * subs + lax.axis_index("sub")
    fold = LANES // pairs
    tiles = c_total // fold
    c_count = c_total // rows
    wide = c_count * cap
    group = out_ref.shape[2]
    main = rows * 256
    share = lax.broadcasted_iota(jnp.int32, (cap, LANES), 1) // pairs
    spot = lax.broadcasted_iota(jnp.int32, (256 + LANES, wide), 0)
    lane = lax.broadcasted_iota(jnp.int32, (1, wide), 1)
    for r in range(rows):
        for i in range(c_count):
            h, j = (r * c_count + i) // tiles, (r * c_count + i) % tiles
            for tile in range(group // LANES):
                whole = None
                for u in range(fold):
                    part = t_ref[tile * fold + u, j * cap : (j + 1) * cap, :]
                    if u != h:
                        part = pltpu.roll(
                            part.astype(jnp.float32), (u - h) * pairs % LANES, 1
                        ).astype(jnp.bfloat16)
                    whole = part if whole is None else jnp.where(share == u, part, whole)
                quarter[i * cap : (i + 1) * cap, tile * LANES : (tile + 1) * LANES] = whole
        for s in range(3):
            target = jnp.full((1, wide), -1, jnp.int32)
            for i in range(c_count):
                c = r * c_count + i
                irrep = jnp.bitwise_xor(irrep_s[c], mine)
                low, high = counts[irrep, 0], counts[irrep + IRREPS, 0]
                spin = s - spin_s[c]
                least = jnp.where(spin == 1, low, 0)
                most = jnp.where(spin == 0, low, jnp.where(spin == 1, low + high, 0))
                place = lane - i * cap
                inside = (place >= least) & (place < most) & (place >= 0) & (place < cap)
                start = offsets[c, mine + 8 * s]
                target = jnp.where(inside, place + (start - least), target)
            over = offsets[c_total + r, mine + 8 * s]
            target = jnp.where(target >= 256, target + over, target)
            part = jnp.dot(
                (target == spot).astype(jnp.bfloat16),
                quarter[...],
                preferred_element_type=jnp.float32,
            )
            out_ref[s, r * 256 : (r + 1) * 256, :] = part[:256].astype(jnp.bfloat16)
            tails[s] = part[256:] if r == 0 else tails[s] + part[256:]
    for s in range(3):
        out_ref[s, main:, :] = tails[s].astype(jnp.bfloat16)


def join_kernel(rows, subs, cap, irrep_s, spin_s, offsets, counts, v_ref, out_ref):
    plane = lax.axis_index("plane")
    mine = lax.axis_index("row") * subs + lax.axis_index("sub")
    c_total = offsets.shape[0] - rows
    half = cap // 2
    main = 2 * cap
    for source in range(rows * subs):
        out_ref[source * main : (source + 1) * main, :] = v_ref[source, :main, :]
    left = lax.broadcasted_iota(jnp.int32, (half, LANES), 1) < 64
    place = lax.broadcasted_iota(jnp.int32, (LANES, LANES), 0) % 64
    lane = lax.broadcasted_iota(jnp.int32, (LANES, LANES), 1)
    slot = lax.broadcasted_iota(jnp.int32, (cap, LANES), 0)
    for y in range(subs):
        a = plane * subs + y
        low = counts[jnp.bitwise_xor(irrep_s[a], mine), 0]
        wide = []
        for r in range(rows):
            tail = v_ref[r * subs + y, main:, :]
            none = jnp.zeros((), tail.dtype)
            wide.append(
                jnp.concatenate(
                    [jnp.where(left, tail, none), jnp.where(left, none, tail)], axis=0
                )
            )
        wide = jnp.concatenate(wide, axis=1)
        joined = []
        for k in range(2):
            places = [
                (place + offsets[c_total + r, mine + 8 * (spin_s[a] + k)] == lane).astype(
                    jnp.bfloat16
                )
                for r in range(rows)
            ]
            joined.append(
                jnp.dot(
                    wide, jnp.concatenate(places, axis=0), preferred_element_type=jnp.float32
                )
            )
        at = rows * subs * main + y * cap
        out_ref[at : at + cap, :] = jnp.where(slot < low, joined[0], joined[1]).astype(
            jnp.bfloat16
        )


def shift_of(k):
    return jnp.where(k % 2 == 1, -((k + 1) // 2), k // 2)


def contract_kernel(rows, planes, subs, first, last, irrep_s, spin_s, counts, t_ref, *refs):
    v_refs = refs[: last - first]
    if first:
        out_hbm, v_rows, out_ref, copied = refs[-4:]
    else:
        out_ref, v_rows = refs[-2:]
    plane = lax.axis_index("plane")
    mine = lax.axis_index("row") * subs + lax.axis_index("sub")
    n, pairs = out_ref.shape[3:]
    main = rows * 256
    for k, v_ref in enumerate(v_refs):
        for y in range(subs):
            top = y * n
            for r in range(rows):
                at = (r * subs + y) * 2 * n
                v_rows[k, top : top + n, r * 256 : r * 256 + 128] = v_ref[at : at + n, :]
                v_rows[k, top : top + n, r * 256 + 128 : (r + 1) * 256] = v_ref[
                    at + n : at + 2 * n, :
                ]
            at = rows * subs * 2 * n + y * n
            v_rows[k, top : top + n, main:] = v_ref[at : at + n, :]
    slot = lax.broadcasted_iota(jnp.int32, (n, rows * pairs), 0)

    def one_plane(k, carry):
        of = lax.rem(plane + shift_of(k + first) + planes, planes)
        for y in range(subs):
            a = of * subs + y
            s = spin_s[a]
            low = counts[jnp.bitwise_xor(irrep_s[a], mine), 0]
            block = v_rows[k, y * n : (y + 1) * n, :]
            lower = jnp.dot(block, t_ref[s], preferred_element_type=jnp.float32)
            upper = jnp.dot(block, t_ref[s + 1], preferred_element_type=jnp.float32)
            result = jnp.where(slot < low, lower, upper).astype(jnp.bfloat16)
            for r in range(rows):
                out_ref[r, k if first else of, y] = result[:, r * pairs : (r + 1) * pairs]
        return carry

    lax.fori_loop(0, last - first, one_plane, 0, unroll=last - first < 4)
    if first:
        for k in range(last - first):
            of = lax.rem(plane + shift_of(k + first) + planes, planes)
            copy = pltpu.make_async_copy(out_ref.at[:, k], out_hbm.at[:, of], copied)
            copy.start()
            copy.wait()


VMEM = pl.BlockSpec(memory_space=pltpu.VMEM)
SMEM = pl.BlockSpec(memory_space=pltpu.SMEM)
ANY = pl.BlockSpec(memory_space=pl.ANY)


def options(limit=24):
    return pltpu.CompilerParams(vmem_limit_bytes=limit * 2**20)


def cost(us):
    return pl.CostEstimate(flops=int(us * 1e9), bytes_accessed=0, transcendentals=0)


def ring_gather(block, planes):
    up = [(i, (i + 1) % planes) for i in range(planes)]
    down = [(i, (i - 1) % planes) for i in range(planes)]
    found = {0: block}
    for step in range(1, planes // 2 + 1):
        found[-step] = lax.ppermute(found[1 - step], "plane", up)
        if 2 * step < planes:
            found[step] = lax.ppermute(found[step - 1], "plane", down)
    return found


def packed(rows, planes, subs, amplitudes, irrep, spin, v_packed, slots, offsets, counts):
    virtuals = irrep.shape[0]
    pairs = amplitudes.shape[0]
    c_total = amplitudes.shape[1] // virtuals
    cap = virtuals // IRREPS * 5 // 4
    group = rows * subs * pairs
    tiles = c_total * pairs // LANES
    plane_axes, all_axes = ("row", "sub"), ("row", "plane", "sub")

    v_plane = lax.all_to_all(v_packed, plane_axes, 0, 0, tiled=True)
    v_plane = pl.pallas_call(
        functools.partial(join_kernel, rows, subs, cap),
        out_shape=jax.ShapeDtypeStruct((subs * cap * (2 * rows + 1), LANES), jnp.bfloat16),
        in_specs=[SMEM] * 4 + [VMEM],
        out_specs=VMEM,
        compiler_params=options(),
        cost_estimate=cost(1.5),
        name="join_tails",
    )(irrep, spin, offsets, counts, v_plane)
    found = ring_gather(v_plane, planes)
    t_packed = pl.pallas_call(
        functools.partial(pack_amplitudes_kernel, c_total, cap),
        out_shape=jax.ShapeDtypeStruct((IRREPS, tiles * cap, LANES), jnp.bfloat16),
        in_specs=[SMEM, VMEM, VMEM],
        out_specs=VMEM,
        scratch_shapes=[
            pltpu.VMEM((c_total * pairs, virtuals), jnp.bfloat16),
            pltpu.VMEM((IRREPS, cap, c_total * pairs), jnp.bfloat16),
        ],
        compiler_params=options(),
        cost_estimate=cost(8),
        name="pack_amplitudes",
    )(irrep, slots, amplitudes)
    t_mine = lax.all_to_all(t_packed, plane_axes, 0, 0, tiled=True)
    t_labels = pl.pallas_call(
        functools.partial(unpack_amplitudes_kernel, rows, subs, c_total, cap, pairs),
        out_shape=jax.ShapeDtypeStruct((3, rows * 256 + LANES, group), jnp.bfloat16),
        in_specs=[SMEM] * 4 + [VMEM],
        out_specs=VMEM,
        scratch_shapes=[
            pltpu.VMEM((c_total // rows * cap, group), jnp.bfloat16),
            pltpu.VMEM((3, LANES, group), jnp.float32),
        ],
        compiler_params=options(),
        cost_estimate=cost(6),
        name="unpack_amplitudes",
    )(irrep, spin, offsets, counts, t_mine)

    shifts = sorted(found, key=abs)
    result = None
    for first, last in ((0, planes - 1), (planes - 1, planes)):
        shape = (rows, planes, subs, cap, group // rows)
        scratch = [
            pltpu.VMEM((last - first, subs * cap, rows * 256 + LANES), jnp.bfloat16),
        ]
        if first:
            scratch += [
                pltpu.VMEM((rows, last - first) + shape[2:], jnp.bfloat16),
                pltpu.SemaphoreType.DMA,
            ]
        blocks = [found[shift] for shift in shifts[first:last]]
        result = pl.pallas_call(
            functools.partial(contract_kernel, rows, planes, subs, first, last),
            out_shape=jax.ShapeDtypeStruct(shape, jnp.bfloat16),
            in_specs=[SMEM] * 3 + [VMEM] * (1 + len(blocks)) + [ANY] * bool(first),
            out_specs=ANY if first else VMEM,
            scratch_shapes=scratch,
            input_output_aliases={4 + len(blocks): 0} if first else {},
            compiler_params=options(),
            cost_estimate=cost(2 * len(blocks)),
            name="contract",
        )(irrep, spin, counts, t_labels, *blocks, *([result] if first else []))
    result = result.reshape(rows * planes * subs, cap, group // rows)
    back = lax.all_to_all(result, all_axes, 0, 0, tiled=True)
    return back


def put_back(rows, planes, subs, back, slots):
    cap, group = back.shape[1], back.shape[2] * rows
    virtuals = slots.shape[1]
    back = back.reshape(rows, planes, subs, cap, group // rows)
    spots = jnp.arange(IRREPS * cap, dtype=jnp.int32)
    rows_back = (spots[:, None] == slots[0]).astype(jnp.bfloat16)
    out = lax.dot_general(
        back,
        rows_back.reshape(rows, subs, cap, virtuals),
        (((0, 2, 3), (0, 1, 2)), ((), ())),
        preferred_element_type=jnp.float32,
    )
    return out.reshape(planes * group // rows, virtuals).astype(jnp.bfloat16)


def local(rows, planes, subs, amplitudes, integrals, irrep, spin):
    virtuals = irrep.shape[0]
    c_count = integrals.shape[1] // virtuals
    c_total = amplitudes.shape[1] // virtuals
    cap = virtuals // IRREPS * 5 // 4
    label_cap = c_count * virtuals // (2 * IRREPS) * 5 // 4
    v_packed, slots, offsets, counts, fits = pl.pallas_call(
        functools.partial(
            pack_integrals_kernel, c_count, c_total, subs, cap, label_cap
        ),
        out_shape=[
            jax.ShapeDtypeStruct((IRREPS, cap * 5 // 2, LANES), jnp.bfloat16),
            jax.ShapeDtypeStruct((2, virtuals), jnp.int32),
            jax.ShapeDtypeStruct((c_total + rows, LANES), jnp.int32),
            jax.ShapeDtypeStruct((2 * IRREPS, LANES), jnp.int32),
            jax.ShapeDtypeStruct((1,), jnp.int32),
        ],
        in_specs=[SMEM, SMEM, VMEM, VMEM, ANY],
        out_specs=[VMEM] * 4 + [SMEM],
        scratch_shapes=[
            pltpu.VMEM((c_count, virtuals, virtuals), jnp.bfloat16),
            pltpu.SemaphoreType.DMA((c_count,)),
            pltpu.VMEM((c_total, LANES), jnp.int32),
            pltpu.VMEM((virtuals, LANES), jnp.float32),
        ],
        compiler_params=options(),
        cost_estimate=cost(9),
        name="pack_integrals",
    )(irrep, spin, irrep[None, :], spin[None, :], integrals)
    back = packed(rows, planes, subs, amplitudes, irrep, spin, v_packed, slots, offsets, counts)
    return lax.cond(
        fits[0] > 0,
        lambda: put_back(rows, planes, subs, back, slots),
        lambda: dense(rows, planes * subs, amplitudes, integrals, irrep, spin),
    )


def solution(mesh):
    rows, cols = mesh.shape["row"], mesh.shape["col"]
    subs = IRREPS // rows
    planes = cols // subs
    split = Mesh(mesh.devices.reshape(rows, planes, subs), ("row", "plane", "sub"))
    col = ("plane", "sub")
    placed = (P(("row",) + col, None), P(col, "row"), P(), P())
    return jax.shard_map(
        functools.partial(local, rows, planes, subs),
        mesh=split,
        in_specs=placed,
        out_specs=P("row", col),
        check_vma=False,
    )
```

```python
import functools

import jax
import jax.numpy as jnp
from jax import lax
from jax.experimental import pallas as pl
from jax.experimental.pallas import tpu as pltpu
from jax.sharding import Mesh, PartitionSpec as P

IRREPS = 8
LANES = 128
NT = (((1,), (1,)), ((), ()))


def pair_labels(lead_irrep, lead_spin, irrep, spin):
    return jnp.bitwise_xor(lead_irrep[:, None], irrep[None, :]) + 8 * (
        lead_spin[:, None] + spin[None, :]
    )


def dense(rows, cols, amplitudes, integrals, irrep, spin):
    virtuals = irrep.shape[0]
    a_count = integrals.shape[0] // virtuals
    c_count = integrals.shape[1] // virtuals
    pairs = amplitudes.shape[0]
    col = ("plane", "sub")

    def labels(first, count):
        return pair_labels(
            lax.dynamic_slice_in_dim(irrep, first, count, 0),
            lax.dynamic_slice_in_dim(spin, first, count, 0),
            irrep,
            spin,
        ).reshape(-1)

    ab_labels = labels(lax.axis_index(col) * a_count, a_count)
    cd_labels = labels(lax.axis_index("row") * c_count, c_count)
    masked = jnp.where(
        ab_labels[:, None] == cd_labels[None, :], integrals, jnp.zeros((), integrals.dtype)
    )
    mine = lax.all_to_all(amplitudes, "row", split_axis=1, concat_axis=0, tiled=True)
    copies = jnp.broadcast_to(mine[None], (cols,) + mine.shape)
    regrouped = lax.all_to_all(copies, col, 0, 0, tiled=True)
    partial_sums = lax.dot_general(
        regrouped.reshape(-1, mine.shape[1]), masked, NT, preferred_element_type=jnp.float32
    )
    partial_sums = partial_sums.reshape(cols, rows, pairs, -1).transpose(1, 0, 2, 3)
    parts = lax.all_to_all(partial_sums, "row", 0, 0, tiled=True)
    return jnp.sum(parts, axis=0).reshape(cols * pairs, -1).astype(jnp.bfloat16)


def pack_integrals_kernel(
    c_count, c_total, subs, cap, label_cap, irrep_s, spin_s, irrep_v, spin_v, v_hbm, *refs
):
    out, slots_out, offsets_out, counts_out, fits_out, v_ref, arrived, ends_ref, tail_ref = refs
    virtuals = v_ref.shape[1]
    copies = []
    for i in range(c_count):
        copies.append(
            pltpu.make_async_copy(
                v_hbm.at[:, i * virtuals : (i + 1) * virtuals], v_ref.at[i], arrived.at[i]
            )
        )
        copies[-1].start()
    row = lax.axis_index("row")
    a = lax.axis_index("plane") * subs + lax.axis_index("sub")
    irrep, spin = irrep_v[...], spin_v[...]
    kinds = 2 * IRREPS
    kind = irrep + IRREPS * spin
    hot = lax.broadcasted_iota(jnp.int32, (kinds, virtuals), 0) == kind
    shape = (virtuals, virtuals)
    upto = lax.broadcasted_iota(jnp.int32, shape, 0) <= lax.broadcasted_iota(jnp.int32, shape, 1)
    blocks = virtuals // LANES
    shape = (LANES, LANES)
    upto = lax.broadcasted_iota(jnp.int32, shape, 0) <= lax.broadcasted_iota(jnp.int32, shape, 1)
    ones = jnp.where(hot, 1.0, 0.0)
    stacked = jnp.concatenate(
        [ones[:, k * LANES : (k + 1) * LANES] for k in range(blocks)], axis=0
    )
    inside = jnp.dot(
        stacked.astype(jnp.bfloat16),
        jnp.where(upto, 1.0, 0.0).astype(jnp.bfloat16),
        preferred_element_type=jnp.float32,
    ).astype(jnp.int32)
    counts = jnp.zeros((kinds, LANES), jnp.int32)
    running = []
    for k in range(blocks):
        block = inside[k * kinds : (k + 1) * kinds] + counts
        running.append(block)
        counts = jnp.broadcast_to(block[:, LANES - 1 :], (kinds, LANES))
    running = jnp.concatenate(running, axis=1)
    counts_out[...] = counts
    rank16 = jnp.sum(jnp.where(hot, running, 0), axis=0, keepdims=True) - 1
    before = jnp.sum(
        jnp.where(hot[IRREPS:], counts[:IRREPS, :1], 0), axis=0, keepdims=True
    )
    rank8 = rank16 + before

    which = lax.broadcasted_iota(jnp.int32, (c_total, LANES), 0)
    lead_irrep = jnp.zeros((c_total, LANES), jnp.int32)
    lead_spin = jnp.zeros((c_total, LANES), jnp.int32)
    for c in range(c_total):
        lead_irrep = jnp.where(which == c, irrep_s[c], lead_irrep)
        lead_spin = jnp.where(which == c, spin_s[c], lead_spin)
    label = lax.broadcasted_iota(jnp.int32, (c_total, LANES), 1)
    d_irrep = jnp.bitwise_xor(label & (IRREPS - 1), lead_irrep)
    d_spin = (label >> 3) - lead_spin
    d_kind = jnp.where((d_spin >= 0) & (d_spin <= 1), d_irrep + IRREPS * d_spin, -1)
    sizes = jnp.zeros((c_total, LANES), jnp.int32)
    for k in range(kinds):
        sizes = jnp.where(d_kind == k, counts[k : k + 1, :], sizes)
    within = lax.broadcasted_iota(jnp.int32, (c_total, LANES), 0) % c_count
    offsets = jnp.zeros((c_total, LANES), jnp.int32)
    for k in range(1, c_count):
        offsets += jnp.where(within >= k, pltpu.roll(sizes, k, 0), 0)
    ends = offsets + sizes
    offsets_out[:c_total, :] = offsets
    ends_ref[...] = ends
    over = jnp.zeros((1, LANES), jnp.int32)
    for r in range(c_total // c_count):
        offsets_out[c_total + r : c_total + r + 1, :] = over
        last = (r + 1) * c_count - 1
        over = over + jnp.maximum(ends[last : last + 1, :] - 256, 0)
    row_label = jnp.bitwise_xor(irrep, irrep_s[a]) + 8 * (spin + spin_s[a])
    row_slot = jnp.bitwise_xor(irrep, irrep_s[a]) * cap + rank8
    slots_out[0:1, :] = row_slot
    slots_out[1:2, :] = irrep * cap + rank8
    which = lax.broadcasted_iota(jnp.int32, (8, LANES), 0)
    first_irrep = jnp.zeros((8, LANES), jnp.int32)
    first_spin = jnp.zeros((8, LANES), jnp.int32)
    start = jnp.zeros((8, LANES), jnp.int32)
    for i in range(c_count):
        c = row * c_count + i
        first_irrep = jnp.where(which == i, irrep_s[c], first_irrep)
        first_spin = jnp.where(which == i, spin_s[c], first_spin)
        start = jnp.where(which == i, offsets_out[pl.ds(c, 1), :], start)
    cd_label = jnp.bitwise_xor(irrep, first_irrep[:, :1]) + 8 * (spin + first_spin[:, :1])
    lines = jnp.broadcast_to(rank16, (8, virtuals))
    for k in range(24):
        lines = lines + jnp.where(cd_label == k, start[:, k : k + 1], 0)
    lines = jnp.where(
        lax.broadcasted_iota(jnp.int32, (8, virtuals), 0) < c_count, lines, row_label
    )
    columns = lines.astype(jnp.float32).T.astype(jnp.int32)
    row_label = columns[:, c_count : c_count + 1]

    tail_ref[...] = jnp.zeros_like(tail_ref)
    lane = lax.broadcasted_iota(jnp.int32, (virtuals, 256), 1)
    tail_lane = 256 + lax.broadcasted_iota(jnp.int32, (virtuals, LANES), 1) % 64
    longest = [jnp.max(ends_ref[pl.ds(row * c_count + i, 1), :]) for i in range(c_count)]
    irrep_most = jnp.max(counts[:IRREPS] + counts[IRREPS:])
    fit = (irrep_most <= cap) & (jnp.max(ends) <= label_cap) & (jnp.max(over) <= LANES)
    fits_out[0] = jnp.where(fit, 1, 0)
    main = None
    for i in range(c_count):
        copies[i].wait()
        masked = jnp.where(
            row_label == cd_label[i : i + 1], v_ref[i], jnp.zeros((), v_ref.dtype)
        )
        slot = columns[:, i : i + 1]
        term = jnp.dot(
            masked, (slot == lane).astype(jnp.bfloat16), preferred_element_type=jnp.float32
        )
        main = term if main is None else main + term

        @pl.when(longest[i] > 256)
        def _(masked=masked, slot=slot):
            tail_ref[...] += jnp.dot(
                masked,
                (slot == tail_lane).astype(jnp.bfloat16),
                preferred_element_type=jnp.float32,
            )

    front = jnp.concatenate([main, tail_ref[...]], axis=1).astype(jnp.bfloat16)
    for g in range(IRREPS):
        spot = lax.broadcasted_iota(jnp.int32, (cap, virtuals), 0) + g * cap
        rows = (row_slot == spot).astype(jnp.bfloat16)
        packed = jnp.dot(rows, front, preferred_element_type=jnp.float32)
        half = cap // 2
        left = lax.broadcasted_iota(jnp.int32, (half, LANES), 1) < 64
        tail = jnp.where(left, packed[:half, 256:], packed[half:, 256:])
        out[g, :cap, :] = packed[:, :128].astype(jnp.bfloat16)
        out[g, cap : 2 * cap, :] = packed[:, 128:256].astype(jnp.bfloat16)
        out[g, 2 * cap :, :] = tail.astype(jnp.bfloat16)


def pack_amplitudes_kernel(c_total, cap, irrep_s, slots, t_ref, out_ref, stacked, moved):
    pairs = t_ref.shape[0]
    virtuals = slots.shape[1]
    fold = LANES // pairs
    tiles = c_total // fold
    for j in range(tiles):
        for h in range(fold):
            c = h * tiles + j
            at = (j * fold + h) * pairs
            stacked[at : at + pairs, :] = t_ref[:, c * virtuals : (c + 1) * virtuals]
    for g in range(IRREPS):
        spot = lax.broadcasted_iota(jnp.int32, (cap, virtuals), 0) + g * cap
        rows = (slots[1:2, :] == spot).astype(jnp.bfloat16)
        moved[g] = lax.dot_general(
            rows, stacked[...], NT, preferred_element_type=jnp.float32
        ).astype(jnp.bfloat16)
    share = lax.broadcasted_iota(jnp.int32, (cap, LANES), 1) // pairs
    for g in range(IRREPS):
        for j in range(tiles):
            tile = None
            for h in range(fold):
                source = jnp.bitwise_xor(irrep_s[h * tiles + j], g)
                part = moved[source, :, j * LANES : (j + 1) * LANES]
                tile = part if tile is None else jnp.where(share == h, part, tile)
            out_ref[g, j * cap : (j + 1) * cap, :] = tile


def unpack_amplitudes_kernel(
    rows, subs, c_total, cap, pairs, irrep_s, spin_s, offsets, counts, t_ref, out_ref, quarter, tails
):
    mine = lax.axis_index("row") * subs + lax.axis_index("sub")
    fold = LANES // pairs
    tiles = c_total // fold
    c_count = c_total // rows
    wide = c_count * cap
    group = out_ref.shape[2]
    main = rows * 256
    share = lax.broadcasted_iota(jnp.int32, (cap, LANES), 1) // pairs
    spot = lax.broadcasted_iota(jnp.int32, (256 + LANES, wide), 0)
    lane = lax.broadcasted_iota(jnp.int32, (1, wide), 1)
    for r in range(rows):
        for i in range(c_count):
            h, j = (r * c_count + i) // tiles, (r * c_count + i) % tiles
            for tile in range(group // LANES):
                whole = None
                for u in range(fold):
                    part = t_ref[tile * fold + u, j * cap : (j + 1) * cap, :]
                    if u != h:
                        part = pltpu.roll(
                            part.astype(jnp.float32), (u - h) * pairs % LANES, 1
                        ).astype(jnp.bfloat16)
                    whole = part if whole is None else jnp.where(share == u, part, whole)
                quarter[i * cap : (i + 1) * cap, tile * LANES : (tile + 1) * LANES] = whole
        for s in range(3):
            target = jnp.full((1, wide), -1, jnp.int32)
            for i in range(c_count):
                c = r * c_count + i
                irrep = jnp.bitwise_xor(irrep_s[c], mine)
                low, high = counts[irrep, 0], counts[irrep + IRREPS, 0]
                spin = s - spin_s[c]
                least = jnp.where(spin == 1, low, 0)
                most = jnp.where(spin == 0, low, jnp.where(spin == 1, low + high, 0))
                place = lane - i * cap
                inside = (place >= least) & (place < most) & (place >= 0) & (place < cap)
                start = offsets[c, mine + 8 * s]
                target = jnp.where(inside, place + (start - least), target)
            over = offsets[c_total + r, mine + 8 * s]
            target = jnp.where(target >= 256, target + over, target)
            part = jnp.dot(
                (target == spot).astype(jnp.bfloat16),
                quarter[...],
                preferred_element_type=jnp.float32,
            )
            out_ref[s, r * 256 : (r + 1) * 256, :] = part[:256].astype(jnp.bfloat16)
            tails[s] = part[256:] if r == 0 else tails[s] + part[256:]
    for s in range(3):
        out_ref[s, main:, :] = tails[s].astype(jnp.bfloat16)


def join_kernel(rows, subs, cap, irrep_s, spin_s, offsets, counts, v_ref, out_ref):
    plane = lax.axis_index("plane")
    mine = lax.axis_index("row") * subs + lax.axis_index("sub")
    c_total = offsets.shape[0] - rows
    half = cap // 2
    main = 2 * cap
    for source in range(rows * subs):
        out_ref[source * main : (source + 1) * main, :] = v_ref[source, :main, :]
    left = lax.broadcasted_iota(jnp.int32, (half, LANES), 1) < 64
    place = lax.broadcasted_iota(jnp.int32, (LANES, LANES), 0) % 64
    lane = lax.broadcasted_iota(jnp.int32, (LANES, LANES), 1)
    slot = lax.broadcasted_iota(jnp.int32, (cap, LANES), 0)
    for y in range(subs):
        a = plane * subs + y
        low = counts[jnp.bitwise_xor(irrep_s[a], mine), 0]
        wide = []
        for r in range(rows):
            tail = v_ref[r * subs + y, main:, :]
            none = jnp.zeros((), tail.dtype)
            wide.append(
                jnp.concatenate(
                    [jnp.where(left, tail, none), jnp.where(left, none, tail)], axis=0
                )
            )
        wide = jnp.concatenate(wide, axis=1)
        joined = []
        for k in range(2):
            places = [
                (place + offsets[c_total + r, mine + 8 * (spin_s[a] + k)] == lane).astype(
                    jnp.bfloat16
                )
                for r in range(rows)
            ]
            joined.append(
                jnp.dot(
                    wide, jnp.concatenate(places, axis=0), preferred_element_type=jnp.float32
                )
            )
        at = rows * subs * main + y * cap
        out_ref[at : at + cap, :] = jnp.where(slot < low, joined[0], joined[1]).astype(
            jnp.bfloat16
        )


def shift_of(k):
    return jnp.where(k % 2 == 1, -((k + 1) // 2), k // 2)


def contract_kernel(rows, planes, subs, first, last, irrep_s, spin_s, counts, t_ref, *refs):
    v_refs = refs[: last - first]
    if first:
        out_hbm, v_rows, out_ref, copied = refs[-4:]
    else:
        out_ref, v_rows = refs[-2:]
    plane = lax.axis_index("plane")
    mine = lax.axis_index("row") * subs + lax.axis_index("sub")
    n, pairs = out_ref.shape[3:]
    main = rows * 256
    for k, v_ref in enumerate(v_refs):
        for y in range(subs):
            top = y * n
            for r in range(rows):
                at = (r * subs + y) * 2 * n
                v_rows[k, top : top + n, r * 256 : r * 256 + 128] = v_ref[at : at + n, :]
                v_rows[k, top : top + n, r * 256 + 128 : (r + 1) * 256] = v_ref[
                    at + n : at + 2 * n, :
                ]
            at = rows * subs * 2 * n + y * n
            v_rows[k, top : top + n, main:] = v_ref[at : at + n, :]
    slot = lax.broadcasted_iota(jnp.int32, (n, rows * pairs), 0)

    def one_plane(k, carry):
        of = lax.rem(plane + shift_of(k + first) + planes, planes)
        for y in range(subs):
            a = of * subs + y
            s = spin_s[a]
            low = counts[jnp.bitwise_xor(irrep_s[a], mine), 0]
            block = v_rows[k, y * n : (y + 1) * n, :]
            lower = jnp.dot(block, t_ref[s], preferred_element_type=jnp.float32)
            upper = jnp.dot(block, t_ref[s + 1], preferred_element_type=jnp.float32)
            result = jnp.where(slot < low, lower, upper).astype(jnp.bfloat16)
            for r in range(rows):
                out_ref[r, k if first else of, y] = result[:, r * pairs : (r + 1) * pairs]
        return carry

    lax.fori_loop(0, last - first, one_plane, 0, unroll=last - first < 4)
    if first:
        for k in range(last - first):
            of = lax.rem(plane + shift_of(k + first) + planes, planes)
            copy = pltpu.make_async_copy(out_ref.at[:, k], out_hbm.at[:, of], copied)
            copy.start()
            copy.wait()


VMEM = pl.BlockSpec(memory_space=pltpu.VMEM)
SMEM = pl.BlockSpec(memory_space=pltpu.SMEM)
ANY = pl.BlockSpec(memory_space=pl.ANY)


def options(limit=24):
    return pltpu.CompilerParams(vmem_limit_bytes=limit * 2**20)


def cost(us):
    return pl.CostEstimate(flops=int(us * 1e9), bytes_accessed=0, transcendentals=0)


def ring_gather(block, planes):
    up = [(i, (i + 1) % planes) for i in range(planes)]
    down = [(i, (i - 1) % planes) for i in range(planes)]
    found = {0: block}
    for step in range(1, planes // 2 + 1):
        found[-step] = lax.ppermute(found[1 - step], "plane", up)
        if 2 * step < planes:
            found[step] = lax.ppermute(found[step - 1], "plane", down)
    return found


def packed(rows, planes, subs, amplitudes, irrep, spin, v_packed, slots, offsets, counts):
    virtuals = irrep.shape[0]
    pairs = amplitudes.shape[0]
    c_total = amplitudes.shape[1] // virtuals
    cap = virtuals // IRREPS * 5 // 4
    group = rows * subs * pairs
    tiles = c_total * pairs // LANES
    plane_axes, all_axes = ("row", "sub"), ("row", "plane", "sub")

    v_plane = lax.all_to_all(v_packed, plane_axes, 0, 0, tiled=True)
    v_plane = pl.pallas_call(
        functools.partial(join_kernel, rows, subs, cap),
        out_shape=jax.ShapeDtypeStruct((subs * cap * (2 * rows + 1), LANES), jnp.bfloat16),
        in_specs=[SMEM] * 4 + [VMEM],
        out_specs=VMEM,
        compiler_params=options(),
        cost_estimate=cost(1.5),
        name="join_tails",
    )(irrep, spin, offsets, counts, v_plane)
    found = ring_gather(v_plane, planes)
    t_packed = pl.pallas_call(
        functools.partial(pack_amplitudes_kernel, c_total, cap),
        out_shape=jax.ShapeDtypeStruct((IRREPS, tiles * cap, LANES), jnp.bfloat16),
        in_specs=[SMEM, VMEM, VMEM],
        out_specs=VMEM,
        scratch_shapes=[
            pltpu.VMEM((c_total * pairs, virtuals), jnp.bfloat16),
            pltpu.VMEM((IRREPS, cap, c_total * pairs), jnp.bfloat16),
        ],
        compiler_params=options(),
        cost_estimate=cost(8),
        name="pack_amplitudes",
    )(irrep, slots, amplitudes)
    t_mine = lax.all_to_all(t_packed, plane_axes, 0, 0, tiled=True)
    t_labels = pl.pallas_call(
        functools.partial(unpack_amplitudes_kernel, rows, subs, c_total, cap, pairs),
        out_shape=jax.ShapeDtypeStruct((3, rows * 256 + LANES, group), jnp.bfloat16),
        in_specs=[SMEM] * 4 + [VMEM],
        out_specs=VMEM,
        scratch_shapes=[
            pltpu.VMEM((c_total // rows * cap, group), jnp.bfloat16),
            pltpu.VMEM((3, LANES, group), jnp.float32),
        ],
        compiler_params=options(),
        cost_estimate=cost(6),
        name="unpack_amplitudes",
    )(irrep, spin, offsets, counts, t_mine)

    shifts = sorted(found, key=abs)
    result = None
    for first, last in ((0, planes - 1), (planes - 1, planes)):
        shape = (rows, planes, subs, cap, group // rows)
        scratch = [
            pltpu.VMEM((last - first, subs * cap, rows * 256 + LANES), jnp.bfloat16),
        ]
        if first:
            scratch += [
                pltpu.VMEM((rows, last - first) + shape[2:], jnp.bfloat16),
                pltpu.SemaphoreType.DMA,
            ]
        blocks = [found[shift] for shift in shifts[first:last]]
        result = pl.pallas_call(
            functools.partial(contract_kernel, rows, planes, subs, first, last),
            out_shape=jax.ShapeDtypeStruct(shape, jnp.bfloat16),
            in_specs=[SMEM] * 3 + [VMEM] * (1 + len(blocks)) + [ANY] * bool(first),
            out_specs=ANY if first else VMEM,
            scratch_shapes=scratch,
            input_output_aliases={4 + len(blocks): 0} if first else {},
            compiler_params=options(),
            cost_estimate=cost(2 * len(blocks)),
            name="contract",
        )(irrep, spin, counts, t_labels, *blocks, *([result] if first else []))
    result = result.reshape(rows * planes * subs, cap, group // rows)
    back = lax.all_to_all(result, all_axes, 0, 0, tiled=True)
    return back


def put_back(rows, planes, subs, back, slots):
    cap, group = back.shape[1], back.shape[2] * rows
    virtuals = slots.shape[1]
    back = back.reshape(rows, planes, subs, cap, group // rows)
    spots = jnp.arange(IRREPS * cap, dtype=jnp.int32)
    rows_back = (spots[:, None] == slots[0]).astype(jnp.bfloat16)
    out = lax.dot_general(
        back,
        rows_back.reshape(rows, subs, cap, virtuals),
        (((0, 2, 3), (0, 1, 2)), ((), ())),
        preferred_element_type=jnp.float32,
    )
    return out.reshape(planes * group // rows, virtuals).astype(jnp.bfloat16)


def local(rows, planes, subs, amplitudes, integrals, irrep, spin):
    virtuals = irrep.shape[0]
    c_count = integrals.shape[1] // virtuals
    c_total = amplitudes.shape[1] // virtuals
    cap = virtuals // IRREPS * 5 // 4
    label_cap = c_count * virtuals // (2 * IRREPS) * 5 // 4
    v_packed, slots, offsets, counts, fits = pl.pallas_call(
        functools.partial(
            pack_integrals_kernel, c_count, c_total, subs, cap, label_cap
        ),
        out_shape=[
            jax.ShapeDtypeStruct((IRREPS, cap * 5 // 2, LANES), jnp.bfloat16),
            jax.ShapeDtypeStruct((2, virtuals), jnp.int32),
            jax.ShapeDtypeStruct((c_total + rows, LANES), jnp.int32),
            jax.ShapeDtypeStruct((2 * IRREPS, LANES), jnp.int32),
            jax.ShapeDtypeStruct((1,), jnp.int32),
        ],
        in_specs=[SMEM, SMEM, VMEM, VMEM, ANY],
        out_specs=[VMEM] * 4 + [SMEM],
        scratch_shapes=[
            pltpu.VMEM((c_count, virtuals, virtuals), jnp.bfloat16),
            pltpu.SemaphoreType.DMA((c_count,)),
            pltpu.VMEM((c_total, LANES), jnp.int32),
            pltpu.VMEM((virtuals, LANES), jnp.float32),
        ],
        compiler_params=options(),
        cost_estimate=cost(9),
        name="pack_integrals",
    )(irrep, spin, irrep[None, :], spin[None, :], integrals)
    back = packed(rows, planes, subs, amplitudes, irrep, spin, v_packed, slots, offsets, counts)
    return lax.cond(
        fits[0] > 0,
        lambda: put_back(rows, planes, subs, back, slots),
        lambda: dense(rows, planes * subs, amplitudes, integrals, irrep, spin),
    )


def solution(mesh):
    rows, cols = mesh.shape["row"], mesh.shape["col"]
    subs = IRREPS // rows
    planes = cols // subs
    split = Mesh(mesh.devices.reshape(rows, planes, subs), ("row", "plane", "sub"))
    col = ("plane", "sub")
    placed = (P(("row",) + col, None), P(col, "row"), P(), P())
    return jax.shard_map(
        functools.partial(local, rows, planes, subs),
        mesh=split,
        in_specs=placed,
        out_specs=P("row", col),
        check_vma=False,
    )
```
